32 devices in a mesh: exp: 8 (over y, x, core), fsdp: 4 (over z).
Axes of the slice: x: 2, y: 2, z: 4, core: 2. Of those that a mesh axis runs over, the one named last changes fastest.
Arguments:
- block_input: bfloat16 [2, 16, 4, 8, 48, 1024], P(None, 'exp', 'fsdp'), may hold values from -6 to 6
- expert_ids: int32 [2, 32, 512, 1], P(None, ('exp', 'fsdp')), may hold values from 0 to 15; in each aligned block of 512 rows (0 to 511, 512 to 1023, ..., all dimensions but the last counted through in order) at most 48 rows name the same one
- seq_lengths: int32 [2, 32], P(None, ('exp', 'fsdp')), may hold values from 64 to 512, as said below
- attn_norm_gain: bfloat16 [1024], P(('exp', 'fsdp')), may hold values from 0.5 to 1.5
- attn_norm_bias: bfloat16 [1024], P(('exp', 'fsdp')), may hold values from -1.25 to 1.25
- query_matrix: bfloat16 [1024, 1024], P(('exp', 'fsdp')), may hold values from -0.1875 to 0.1875
- query_offset_bias: bfloat16 [1024], P(('exp', 'fsdp')), may hold values from -1.25 to 1.25
- key_matrix: bfloat16 [1024, 1024], P(('exp', 'fsdp')), may hold values from -0.1875 to 0.1875
- value_matrix: bfloat16 [1024, 1024], P(('exp', 'fsdp')), may hold values from -0.1875 to 0.1875
- value_offset_bias: bfloat16 [1024], P(('exp', 'fsdp')), may hold values from -1.25 to 1.25
- output_matrix: bfloat16 [1024, 1024], P(('exp', 'fsdp')), may hold values from -0.75 to 0.75
- attention_output_bias: bfloat16 [1024], P(('exp', 'fsdp')), may hold values from -0.625 to 0.625
- ffn_norm_gain: bfloat16 [1024], P(('exp', 'fsdp')), may hold values from 0.5 to 1.5
- ffn_norm_bias: bfloat16 [1024], P(('exp', 'fsdp')), may hold values from -1.25 to 1.25
- expert_in: bfloat16 [16, 1024, 4096], P('exp', None, 'fsdp'), may hold values from -0.1875 to 0.1875
- expert_in_bias: bfloat16 [16, 4096], P('exp', 'fsdp'), may hold values from -0.625 to 0.625
- expert_out: bfloat16 [16, 4096, 1024], P('exp', 'fsdp'), may hold values from -0.09375 to 0.09375
- expert_out_bias: bfloat16 [16, 1024], P('exp', 'fsdp'), may hold values from -0.625 to 0.625
- out_cotangent: bfloat16 [2, 16, 4, 8, 48, 1024], P(None, 'exp', 'fsdp'), may hold values from -6 to 6
Outputs:
- block_output: bfloat16 [2, 16, 4, 8, 48, 1024], P(None, 'exp', 'fsdp')
- input_grad: bfloat16 [2, 16, 4, 8, 48, 1024], P(None, 'exp', 'fsdp')
- grad_attn_gain: float32 [1024], P(('exp', 'fsdp'))
- grad_attn_bias: float32 [1024], P(('exp', 'fsdp'))
- grad_query: float32 [1024, 1024], P(('exp', 'fsdp'))
- grad_query_bias: float32 [1024], P(('exp', 'fsdp'))
- grad_key: float32 [1024, 1024], P(('exp', 'fsdp'))
- grad_value: float32 [1024, 1024], P(('exp', 'fsdp'))
- grad_value_bias: float32 [1024], P(('exp', 'fsdp'))
- grad_output: float32 [1024, 1024], P(('exp', 'fsdp'))
- grad_output_bias: float32 [1024], P(('exp', 'fsdp'))
- grad_ffn_gain: float32 [1024], P(('exp', 'fsdp'))
- grad_ffn_bias: float32 [1024], P(('exp', 'fsdp'))
- grad_expert_in: float32 [16, 1024, 4096], P('exp', None, 'fsdp')
- grad_expert_in_bias: float32 [16, 4096], P('exp', 'fsdp')
- grad_expert_out: float32 [16, 4096, 1024], P('exp', 'fsdp')
- grad_expert_out_bias: float32 [16, 1024], P('exp', 'fsdp')
The draws below stay inside these ranges and needn't reach their ends.
Inputs may be any that keep to these rules, and one draw needn't show every extreme that they name: `expert_ids`: in each sequence no expert is named by more than 48 positions, and in every draw some expert is named by exactly 48 positions of some sequence. `seq_lengths`: in each micro-batch one sequence, drawn from the seed, has length 512.
All inputs are finite; a program needn't handle non-finite values.
Results may differ from the reference program's by a relative error of at most 0.014.
Values may be sent and summed in bfloat16 or wider, within the bound.
No kernel may reach another device: no remote copies, remote signals or barrier semaphores. Data moves between devices by JAX's collectives and lax.ppermute only.
A program may use at most 384 MiB of HBM per device.

```python
import math
import jax
import jax.numpy as jnp
import numpy as np
from jax import lax

D = 1024
HEADS = 16
HEAD_DIM = 64
FF = 4096
EXPERTS = 16
SEQ = 512
MIN_LEN = 64
MB = 2
SEQS = 32
CAPE = 48
N_EXP = 8
N_FSDP = 4


def draw_seq_lengths(key, part):
    key_len, key_top = jax.random.split(key)
    lengths_drawn = jax.random.randint(key_len, (MB, SEQS), MIN_LEN, SEQ + 1, dtype=jnp.int32)
    longest = jax.random.randint(key_top, (MB, 1), 0, SEQS, dtype=jnp.int32)
    positions = jnp.arange(SEQS, dtype=jnp.int32)[None, :]
    return jnp.where(positions == longest, SEQ, lengths_drawn).astype(jnp.int32)


def block_levels(stream_key, extent, cuts, least, high):
    loudness, own = 1.0, jax.random.fold_in(stream_key, 6)
    for axis_at, shards_of in cuts:
        heights = jnp.exp(jax.random.uniform(jax.random.fold_in(own, axis_at), (shards_of,), jnp.float32, least / len(cuts), high / len(cuts)))
        loudness = loudness * jnp.repeat(heights, extent[axis_at] // shards_of).reshape([-1 if axis == axis_at else 1 for axis in range(len(extent))])
    return loudness


def deal_out(own_key, own, number, rows, number_of, top, limit, slope):
    ranking = jax.random.permutation(own_key, number_of)
    heavy_load, ordinary = portions_of(number_of, rows * top, limit, slope, True), portions_of(number_of, rows * top, limit, slope, False)
    places = jnp.arange(number_of)

    def named(sizes, turn):
        used = int((sizes > 0).sum())
        fixed = max(1, used // 4)
        moved = fixed + (places - fixed + turn * (used - fixed)) % max(1, number_of - fixed)
        return jnp.zeros((number_of,), jnp.int32).at[ranking[jnp.where(places < fixed, places, moved)]].set(jnp.asarray(sizes, jnp.int32))

    sizes = jnp.where(number % 4 == 0, named(heavy_load, number // 4), named(ordinary, number - number // 4 - 1))
    mixed = jax.random.permutation(jax.random.fold_in(own, 3), number_of)
    giver, taker = mixed[0:number_of // 2 * 2:2], mixed[1:number_of // 2 * 2:2]
    slack = jnp.minimum(sizes[giver] - 1, limit - sizes[taker]) // 2
    slack = jnp.where((giver == ranking[0]) | (taker == ranking[0]) | (sizes[taker] == 0), 0, jnp.maximum(slack, 0))
    moved = jax.random.randint(jax.random.fold_in(own, 4), (number_of // 2,), 0, 1 << 20) % (slack + 1)
    sizes = sizes.at[giver].add(-moved).at[taker].add(moved)
    labels = jnp.searchsorted(jnp.cumsum(sizes), jnp.arange(rows * top), side="right").astype(jnp.int32)
    grid = labels.reshape(top, rows).T
    grid = grid[jax.random.permutation(jax.random.fold_in(own, 1), rows)]
    turn = jax.random.randint(jax.random.fold_in(own, 2), (rows, 1), 0, top)
    return jnp.take_along_axis(grid, (jnp.arange(top)[None, :] + turn) % top, axis=1)


def portions_of(count, total, reach, lean, full):
    weights = [(1 << 20) // math.isqrt(standing ** lean) + 1 for standing in range(1, count + 1)]
    largest = reach if full else min(reach, max(-(-total // count), total * weights[0] // sum(weights)))
    least = 1 if total - largest >= count - 1 else 0
    holding, surplus = [largest] + [least] * (count - 1), total - largest - least * (count - 1)
    while surplus > 0:
        candidates = [i for i in range(1, count) if holding[i] < largest] or [i for i in range(1, count) if holding[i] < reach]
        pool, remaining = sum([weights[i] for i in candidates]), surplus
        for i in candidates:
            extra = min(reach - holding[i], max(1, remaining * weights[i] // pool), surplus)
            holding[i] = holding[i] + extra
            surplus = surplus - extra
    return np.array(holding)


def scatter_about(own_key, dims, spread, reach, cuts=(), held_as=jnp.bfloat16):
    level = block_levels(own_key, dims, cuts, -0.22, 0.18) if cuts else 1.0
    values = jax.random.normal(own_key, dims, jnp.float32) * spread * level
    return jnp.minimum(jnp.maximum(values, -reach), reach).astype(held_as)


def setup_inputs(seed: int = 0) -> dict:
    key_list = jax.random.split(jax.random.key(seed), 20)
    block_input = scatter_about(key_list[0], (MB, EXPERTS, N_FSDP, N_EXP, CAPE, D), 1.0, 6.0, ((1, 8), (2, 4)))
    expert_ids_keys = jax.random.split(jax.random.fold_in(key_list[1], 1), MB * SEQS * SEQ // SEQ)
    expert_ids_turns = jax.random.permutation(jax.random.fold_in(key_list[1], 3), MB * SEQS * SEQ // SEQ)
    expert_ids = jax.vmap(lambda own, number: deal_out(jax.random.fold_in(key_list[1], 2), own, number, SEQ, EXPERTS, 1, CAPE, 1))(expert_ids_keys, expert_ids_turns).reshape((MB, SEQS, SEQ, 1))
    seq_lengths = draw_seq_lengths(jax.random.fold_in(key_list[19], 71), 0)
    attn_norm_gain = jnp.clip(1.0 + 0.1 * jax.random.normal(key_list[3], (D,), jnp.float32), 0.5, 1.5).astype(jnp.bfloat16)
    attn_norm_bias = scatter_about(key_list[4], (D,), 0.2, 1.25, ((0, 32),))
    query_matrix = scatter_about(key_list[5], (D, D), D ** -0.5, 0.1875, ((0, 32),))
    query_offset_bias = scatter_about(key_list[6], (D,), 0.2, 1.25, ((0, 32),))
    key_matrix = scatter_about(key_list[7], (D, D), D ** -0.5, 0.1875, ((0, 32),))
    value_matrix = scatter_about(key_list[8], (D, D), D ** -0.5, 0.1875, ((0, 32),))
    value_offset_bias = scatter_about(key_list[9], (D,), 0.2, 1.25, ((0, 32),))
    output_matrix = scatter_about(key_list[10], (D, D), (D // 16) ** -0.5, 0.75, ((0, 32),))
    attention_output_bias = scatter_about(key_list[11], (D,), 0.1, 0.625, ((0, 32),))
    ffn_norm_gain = jnp.clip(1.0 + 0.1 * jax.random.normal(key_list[12], (D,), jnp.float32), 0.5, 1.5).astype(jnp.bfloat16)
    ffn_norm_bias = scatter_about(key_list[13], (D,), 0.2, 1.25, ((0, 32),))
    expert_in = scatter_about(key_list[14], (EXPERTS, D, FF), D ** -0.5, 0.1875, ((0, 8), (2, 4)))
    expert_in_bias = scatter_about(key_list[15], (EXPERTS, FF), 0.1, 0.625, ((0, 8), (1, 4)))
    expert_out = scatter_about(key_list[16], (EXPERTS, FF, D), FF ** -0.5, 0.09375, ((0, 8), (1, 4)))
    expert_out_bias = scatter_about(key_list[17], (EXPERTS, D), 0.1, 0.625, ((0, 8), (1, 4)))
    out_cotangent = scatter_about(key_list[18], (MB, EXPERTS, N_FSDP, N_EXP, CAPE, D), 1.0, 6.0, ((1, 8), (2, 4)))
    return dict(block_input=block_input, expert_ids=expert_ids, seq_lengths=seq_lengths, attn_norm_gain=attn_norm_gain, attn_norm_bias=attn_norm_bias, query_matrix=query_matrix, query_offset_bias=query_offset_bias, key_matrix=key_matrix, value_matrix=value_matrix, value_offset_bias=value_offset_bias, output_matrix=output_matrix, attention_output_bias=attention_output_bias, ffn_norm_gain=ffn_norm_gain, ffn_norm_bias=ffn_norm_bias, expert_in=expert_in, expert_in_bias=expert_in_bias, expert_out=expert_out, expert_out_bias=expert_out_bias, out_cotangent=out_cotangent)


@jax.custom_vjp
def low(v):
    return lax.optimization_barrier(v.astype(jnp.bfloat16)).astype(jnp.float32)

@jax.custom_vjp
def low_back(v):
    return v

def low_keep(v):
    return (low(v), None)

def low_pass(kept, grad):
    return (grad,)

def back_keep(v):
    return (v, None)

def back_low(kept, grad):
    return (low(grad),)
low.defvjp(low_keep, low_pass)
low_back.defvjp(back_keep, back_low)
precision_highest = lax.Precision.HIGHEST

def bidirectional_view(inputs):
    return low_back(low(inputs))

def layer_norm(inputs, norm_gain, norm_bias):
    average = lax.optimization_barrier(jnp.mean(inputs, axis=-1, keepdims=True))
    centred = inputs - average
    variance = lax.optimization_barrier(jnp.mean(centred * centred, axis=-1, keepdims=True))
    return centred * lax.rsqrt(variance + 1e-05) * norm_gain + norm_bias

def smooth_gate(inputs):
    return jax.nn.gelu(inputs, approximate=True)

def attend_group(pieces):
    query_rows, keys_in, values_in, lengths = pieces
    scaling = HEAD_DIM ** (-0.5)
    scores = low_back(jnp.einsum('gqhd,gkhd->ghqk', query_rows, keys_in, precision=precision_highest) * scaling)
    query_pos = jnp.arange(SEQ, dtype=jnp.int32)[:, None]
    key_pos = jnp.arange(SEQ, dtype=jnp.int32)[None, :]
    allowed = (key_pos <= query_pos)[None, None] & (key_pos[None, None] < lengths[:, None, None, None])
    scores = jnp.where(allowed, scores, -1e+30)
    row_max = lax.optimization_barrier(jnp.max(scores, axis=-1, keepdims=True))
    weights = jnp.exp(scores - row_max)
    attn_probs = weights / lax.optimization_barrier(jnp.sum(weights, axis=-1, keepdims=True))
    return jnp.einsum('ghqk,gkhd->gqhd', low(attn_probs), values_in, precision=precision_highest)

def expert_ffn(pieces):
    normalized_rows, w_first, b_first, w_second, b_second = pieces
    inner_pre = low_back(jnp.dot(normalized_rows, w_first, precision=precision_highest) + b_first)
    activated = low(smooth_gate(inner_pre))
    return jnp.dot(activated, w_second, precision=precision_highest) + b_second

def micro_step(inputs, params, expert_row, rank_in, lengths, filled):
    attn_gain, attn_shift, query_matrix, query_offset_bias, key_matrix, value_matrix, value_offset_bias, output_matrix, attention_output_bias, ffn_gain, ffn_shift, expert_in, expert_in_bias, expert_out, expert_out_bias = params
    seq_ids = jnp.arange(SEQS, dtype=jnp.int32)[:, None]
    seq_exp = seq_ids // N_FSDP
    seq_grp = seq_ids % N_FSDP
    gathered = low_back(inputs[expert_row, seq_grp, seq_exp, rank_in])
    normalized_rows = low(layer_norm(gathered, attn_gain, attn_shift))
    query_rows = bidirectional_view(jnp.einsum('gpc,cy->gpy', normalized_rows, query_matrix, precision=precision_highest) + query_offset_bias)
    key_rows_total = bidirectional_view(jnp.einsum('gpc,cy->gpy', normalized_rows, key_matrix, precision=precision_highest))
    value_rows_total = bidirectional_view(jnp.einsum('gpc,cy->gpy', normalized_rows, value_matrix, precision=precision_highest) + value_offset_bias)
    group_size = math.gcd(SEQS, max(1, 4096 // SEQ))

    def split_heads(tensor):
        return tensor.reshape(SEQS // group_size, group_size, SEQ, HEADS, HEAD_DIM)
    attention_result = lax.map(jax.checkpoint(attend_group), (split_heads(query_rows), split_heads(key_rows_total), split_heads(value_rows_total), lengths.reshape(SEQS // group_size, group_size)))
    attention_result = bidirectional_view(attention_result.reshape(SEQS, SEQ, D))
    attention_output = bidirectional_view(jnp.einsum('gpc,cy->gpy', attention_result, output_matrix, precision=precision_highest) + attention_output_bias)
    placed = jnp.zeros(inputs.shape, jnp.float32).at[expert_row, seq_grp, seq_exp, rank_in].set(attention_output)
    slot_count = N_FSDP * N_EXP * CAPE
    mixed_rows = (inputs + placed).reshape(EXPERTS, slot_count, D)
    ffn_in = low(layer_norm(mixed_rows, ffn_gain, ffn_shift))
    ffn_out = lax.map(jax.checkpoint(expert_ffn), (ffn_in, expert_in, expert_in_bias, expert_out, expert_out_bias))
    result = jnp.where(filled.reshape(EXPERTS, slot_count, 1) > 0.5, mixed_rows + ffn_out, 0.0)
    return result.reshape(inputs.shape)

def reference(block_input, expert_ids, seq_lengths, attn_norm_gain, attn_norm_bias, query_matrix, query_offset_bias, key_matrix, value_matrix, value_offset_bias, output_matrix, attention_output_bias, ffn_norm_gain, ffn_norm_bias, expert_in, expert_in_bias, expert_out, expert_out_bias, out_cotangent):
    expert_all = expert_ids[..., 0]
    onehot = (expert_all[..., None] == jnp.arange(EXPERTS, dtype=jnp.int32)).astype(jnp.int32)
    before = (jnp.cumsum(onehot, axis=2) - onehot).astype(jnp.int32)
    rank_in = lax.optimization_barrier(jnp.sum(before * onehot, axis=3)).astype(jnp.int32)
    counts = lax.optimization_barrier(jnp.sum(onehot, axis=2)).astype(jnp.int32)
    per_group = counts.reshape(MB, N_EXP, N_FSDP, EXPERTS).transpose(0, 3, 2, 1)
    filled = (jnp.arange(CAPE, dtype=jnp.int32) < per_group[..., None]).astype(jnp.float32)
    params = tuple((member.astype(jnp.float32) for member in (attn_norm_gain, attn_norm_bias, query_matrix, query_offset_bias, key_matrix, value_matrix, value_offset_bias, output_matrix, attention_output_bias, ffn_norm_gain, ffn_norm_bias, expert_in, expert_in_bias, expert_out, expert_out_bias)))

    def forward(inputs_all, weights_all):
        outputs = []
        for micro_idx in range(MB):
            checkpointed = jax.checkpoint(micro_step)
            outputs.append(checkpointed(inputs_all[micro_idx], weights_all, expert_all[micro_idx], rank_in[micro_idx], seq_lengths[micro_idx], filled[micro_idx]))
        return jnp.stack(outputs)
    inputs_full = block_input.astype(jnp.float32)
    out_full, pullback = jax.vjp(forward, inputs_full, params)
    grad_input, grad_params = pullback(out_cotangent.astype(jnp.float32))
    return (out_full.astype(jnp.bfloat16), grad_input.astype(jnp.bfloat16), grad_params[0], grad_params[1], grad_params[2], grad_params[3], grad_params[4], grad_params[5], grad_params[6], grad_params[7], grad_params[8], grad_params[9], grad_params[10], grad_params[11], grad_params[12], grad_params[13], grad_params[14])
```

```python
import jax
import jax.numpy as jnp
from jax import lax
from jax.sharding import PartitionSpec as P

HEADS = 16
BF = jnp.bfloat16
F32 = jnp.float32


def norm_parts(inputs):
    average = jnp.mean(inputs, axis=-1, keepdims=True)
    centred = inputs - average
    variance = jnp.mean(centred * centred, axis=-1, keepdims=True)
    inverse = lax.rsqrt(variance + 1e-05)
    return (centred * inverse, inverse)


def norm_back(grad_normed, normal, inverse, norm_gain):
    scaled = grad_normed * norm_gain
    return inverse * (
        scaled
        - jnp.mean(scaled, axis=-1, keepdims=True)
        - normal * jnp.mean(scaled * normal, axis=-1, keepdims=True)
    )


def smooth_gate(inputs):
    return jax.nn.gelu(inputs, approximate=True)


def dot(a, b, dims):
    return lax.dot_general(a, b, (dims, ((), ())), preferred_element_type=F32)


def split_heads(tensor):
    return tensor.reshape(tensor.shape[0], HEADS, tensor.shape[1] // HEADS)


def block_scores(query_heads, key_heads, length, scaling):
    n = key_heads.shape[0]
    key_pos = jnp.arange(n, dtype=jnp.int32)[None, None, :]
    query_pos = jnp.arange(n, dtype=jnp.int32)[None, :, None]
    allowed = (key_pos <= query_pos) & (key_pos < length)
    scores = (
        jnp.einsum("qhd,khd->hqk", query_heads, key_heads, preferred_element_type=F32)
        * scaling
    )
    return jnp.where(allowed, scores, -1e30)


def attend_forward(q, k, v, length):
    seq_len, width = q.shape
    scaling = (width // HEADS) ** (-0.5)
    scores = block_scores(split_heads(q), split_heads(k), length, scaling)
    row_max = jnp.max(scores, axis=-1, keepdims=True)
    weights = jnp.exp(scores - row_max)
    row_total = jnp.sum(weights, axis=-1, keepdims=True)
    probs = (weights / row_total).astype(BF)
    out = jnp.einsum("hqk,khd->qhd", probs, split_heads(v), preferred_element_type=F32)
    return out.reshape(seq_len, width).astype(BF), row_max + jnp.log(row_total)


def attend_backward(q, k, v, length, lse, grad_attended):
    seq_len, width = q.shape
    scaling = (width // HEADS) ** (-0.5)
    qh, kh, vh, gh = (split_heads(a) for a in (q, k, v, grad_attended))
    probs = jnp.exp(block_scores(qh, kh, length, scaling) - lse)
    grad_probs = jnp.einsum("qhd,khd->hqk", gh, vh, preferred_element_type=F32)
    inner_sum = jnp.sum(probs * grad_probs, axis=-1, keepdims=True)
    grad_scores = (probs * (grad_probs - inner_sum)).astype(BF)
    dq = jnp.einsum("hqk,khd->qhd", grad_scores, kh, preferred_element_type=F32) * scaling
    dk = jnp.einsum("hqk,qhd->khd", grad_scores, qh, preferred_element_type=F32) * scaling
    dv = jnp.einsum("hqk,qhd->khd", probs.astype(BF), gh, preferred_element_type=F32)
    return tuple(a.reshape(seq_len, width).astype(BF) for a in (dq, dk, dv))


def attention_forward(arrived, slot_ids, length, dense, small):
    rows = arrived[slot_ids]
    normal, _ = norm_parts(rows.astype(F32))
    normed = (normal * small[0] + small[1]).astype(BF)
    q = (dot(normed, dense[0], ((1,), (0,))) + small[2]).astype(BF)
    k = dot(normed, dense[1], ((1,), (0,))).astype(BF)
    v = (dot(normed, dense[2], ((1,), (0,))) + small[3]).astype(BF)
    attended, lse = attend_forward(q, k, v, length)
    out = (dot(attended, dense[3], ((1,), (0,))) + small[4]).astype(BF)
    placed = jnp.zeros(arrived.shape, BF).at[slot_ids].set(out)
    return placed, (rows, q, k, v, attended, lse)


def attention_backward(grad_arrived, slot_ids, length, dense, small, saved):
    rows, q, k, v, attended, lse = saved
    normal, inverse = norm_parts(rows.astype(F32))
    normed = (normal * small[0] + small[1]).astype(BF)
    grad_out = grad_arrived[slot_ids]
    dwo = dot(attended, grad_out, ((0,), (0,)))
    dbo = jnp.sum(grad_out.astype(F32), axis=0)
    grad_attended = dot(grad_out, dense[3], ((1,), (1,))).astype(BF)
    dq, dk, dv = attend_backward(q, k, v, length, lse, grad_attended)
    dws = [dot(normed, a, ((0,), (0,))) for a in (dq, dk, dv)] + [dwo]
    grad_normed = sum(dot(a, w, ((1,), (1,))) for a, w in zip((dq, dk, dv), dense))
    smalls = [
        jnp.sum(grad_normed * normal, axis=0),
        jnp.sum(grad_normed, axis=0),
        jnp.sum(dq.astype(F32), axis=0),
        jnp.sum(dv.astype(F32), axis=0),
        dbo,
    ]
    back = norm_back(grad_normed, normal, inverse, small[0]).astype(BF)
    placed = jnp.zeros(grad_arrived.shape, BF).at[slot_ids].set(back)
    return placed, dws, smalls


def expert_step(x, g, w_in, b_in, w_out):
    inner = dot(x, w_in, ((1,), (0,))) + b_in[None, :]
    activated, pull = jax.vjp(smooth_gate, inner)
    activated = activated.astype(BF)
    out = dot(activated, w_out, ((1,), (0,))).astype(BF)
    grad_act = dot(g, w_out, ((1,), (1,)))
    grad_inner = pull(grad_act)[0].astype(BF)
    grad_x = dot(grad_inner, w_in, ((1,), (1,))).astype(BF)
    dw_in = dot(x, grad_inner, ((0,), (0,)))
    dw_out = dot(activated, g, ((0,), (0,)))
    db_in = jnp.sum(grad_inner.astype(F32), axis=0)
    return out, grad_x, dw_in, dw_out, db_in


def reduce_dense(parts, n_exp, n_f, ex, fi):
    rows, width = parts.shape[1:]
    chips = n_exp // 2
    chip, core = ex // 2, ex % 2
    view = parts.reshape(chips, 2, n_f * rows, width)
    keep = lax.dynamic_index_in_dim(view, core, 1, keepdims=False)
    give = lax.dynamic_index_in_dim(view, 1 - core, 1, keepdims=False)
    got = lax.ppermute(give, "exp", [(i, i ^ 1) for i in range(n_exp)])
    summed = keep + got
    low = summed.astype(BF)
    total = lax.dynamic_index_in_dim(summed, chip, 0, keepdims=False)
    for step in range(1, chips):
        block = lax.dynamic_index_in_dim(low, chip ^ step, 0, keepdims=False)
        total = total + lax.ppermute(
            block, "exp", [(i, i ^ (2 * step)) for i in range(n_exp)]
        ).astype(F32)
    total = total.reshape(n_f, rows, width)
    half = n_f // 2
    while half >= 1:
        pairs = total.reshape(2, half, rows, width)
        side = (fi // half) % 2
        give = lax.dynamic_index_in_dim(pairs, 1 - side, 0, keepdims=False)
        keep = lax.dynamic_index_in_dim(pairs, side, 0, keepdims=False)
        total = keep + lax.ppermute(
            give.astype(BF), "fsdp", [(i, i ^ half) for i in range(n_f)]
        ).astype(F32)
        half //= 2
    return total.reshape(rows, width)


def body(
    block_input,
    expert_ids,
    seq_lengths,
    attn_norm_gain,
    attn_norm_bias,
    query_matrix,
    query_offset_bias,
    key_matrix,
    value_matrix,
    value_offset_bias,
    output_matrix,
    attention_output_bias,
    ffn_norm_gain,
    ffn_norm_bias,
    expert_in,
    expert_in_bias,
    expert_out,
    expert_out_bias,
    out_cotangent,
):
    mb, le, _, sources, cap, width = block_input.shape
    n_exp, n_f = lax.axis_size("exp"), lax.axis_size("fsdp")
    ex, fi = lax.axis_index("exp"), lax.axis_index("fsdp")
    everyone = ("exp", "fsdp")
    experts = le * n_exp
    slots = experts * cap
    rows = sources * cap
    hidden = expert_in.shape[2]
    seq = expert_ids.shape[2]
    far = [(i, i ^ 2) for i in range(n_f)]
    near = [(i, i ^ 1) for i in range(n_f)]
    share = attn_norm_gain.shape[0]

    dense_full = lax.all_gather(
        jnp.stack([query_matrix, key_matrix, value_matrix, output_matrix]), everyone, axis=1, tiled=True
    )
    ids = expert_ids[:, 0, :, 0]
    onehot = ids[:, :, None] == jnp.arange(experts, dtype=jnp.int32)
    counts = jnp.sum(onehot.astype(F32), axis=1)
    position = jnp.arange(seq, dtype=jnp.int32)
    same = (ids[:, :, None] == ids[:, None, :]) & (position[None, None, :] < position[None, :, None])
    slot_ids = ids * cap + jnp.sum(same.astype(jnp.int32), axis=2)

    packed = jnp.concatenate(
        [
            attn_norm_gain,
            attn_norm_bias,
            query_offset_bias,
            value_offset_bias,
            attention_output_bias,
            ffn_norm_gain,
            ffn_norm_bias,
            expert_out_bias.reshape(-1),
            expert_in_bias.reshape(-1),
            counts.astype(BF).reshape(-1),
        ]
    )
    table = lax.all_gather(packed[None], everyone, axis=0, tiled=True).astype(F32)
    small = [table[:, i * share : (i + 1) * share].reshape(-1) for i in range(7)]
    at = 7 * share
    table = table.reshape(n_exp, n_f, -1)
    mine = lax.dynamic_index_in_dim(table, ex, 0, keepdims=False)
    bias_out = mine[:, at : at + expert_out_bias.size].reshape(n_f, le, -1).transpose(1, 0, 2).reshape(le, width)
    at += expert_out_bias.size
    bias_in = mine[:, at : at + le * hidden].reshape(n_f, le, hidden)
    bias_in = jnp.concatenate(
        [
            lax.dynamic_index_in_dim(bias_in, fi, 0, keepdims=False),
            lax.dynamic_index_in_dim(bias_in, fi ^ 1, 0, keepdims=False),
        ],
        axis=1,
    )
    at += le * hidden
    all_counts = table[:, :, at:].reshape(n_exp, n_f, mb, n_exp, le)
    my_counts = lax.dynamic_index_in_dim(all_counts, ex, 3, keepdims=False)

    def fill(group):
        count = lax.dynamic_index_in_dim(my_counts, group, 1, keepdims=False)
        count = count.transpose(1, 2, 0)[:, :, :, None]
        return (jnp.arange(cap, dtype=F32) < count).astype(F32).reshape(mb, le, rows, 1)

    fill_own, fill_far = fill(fi), fill(fi ^ 2)

    arrived_all = lax.all_to_all(
        block_input[:, :, 0], "exp", split_axis=2, concat_axis=1, tiled=True
    ).reshape(mb, slots, width)

    w_in = jnp.concatenate([expert_in, lax.ppermute(expert_in, "fsdp", near)], axis=2)
    w_out = jnp.concatenate([expert_out, lax.ppermute(expert_out, "fsdp", near)], axis=1)

    cot = out_cotangent[:, :, 0].reshape(mb, le, rows, width)
    cot_far = [lax.ppermute(cot[t], "fsdp", far) for t in range(mb)]

    outputs, input_grads = [], []
    dense_total, small_total, expert_total = None, None, None
    for t in range(mb):
        placed, saved = attention_forward(arrived_all[t], slot_ids[t], seq_lengths[t, 0], dense_full, small)
        back_rows = lax.all_to_all(
            placed.reshape(experts, cap, width), "exp", split_axis=0, concat_axis=1, tiled=True
        ).reshape(le, rows, width)
        mixed = block_input[t, :, 0].reshape(le, rows, width).astype(F32) + back_rows.astype(F32)
        normal_two, inverse_two = norm_parts(mixed)
        normed_two = (normal_two * small[5] + small[6]).astype(BF)
        normed_far = lax.ppermute(normed_two, "fsdp", far)
        grad_rows = cot[t] * fill_own[t].astype(BF)
        grad_far = cot_far[t] * fill_far[t].astype(BF)
        outs, gxs, dwi, dwo, dbi = [], [], [], [], []
        for j in range(le):
            x = jnp.concatenate([normed_two[j], normed_far[j]], axis=0)
            g = jnp.concatenate([grad_rows[j], grad_far[j]], axis=0)
            out, gx, a, b, c = expert_step(x, g, w_in[j], bias_in[j], w_out[j])
            outs.append(out)
            gxs.append(gx)
            dwi.append(a)
            dwo.append(b)
            dbi.append(c)
        gx_all = jnp.stack(gxs)
        grad_normed = gx_all[:, :rows].astype(F32) + lax.ppermute(gx_all[:, rows:], "fsdp", far).astype(F32)
        out_all = jnp.stack(outs)
        ffn_out = out_all[:, :rows].astype(F32) + lax.ppermute(out_all[:, rows:], "fsdp", far).astype(F32)
        ffn_out = ffn_out + bias_out[:, None, :]
        outputs.append(
            ((mixed + ffn_out) * fill_own[t]).astype(BF).reshape(le, 1, sources, cap, width)
        )
        dbo = jnp.sum(grad_rows.astype(F32), axis=1) + jnp.sum(grad_far.astype(F32), axis=1)
        grad_mixed = grad_rows.astype(F32) + norm_back(grad_normed, normal_two, inverse_two, small[5])
        grad_arrived = lax.all_to_all(
            grad_mixed.astype(BF).reshape(le, sources, cap, width), "exp", split_axis=1, concat_axis=0, tiled=True
        ).reshape(slots, width)
        placed_back, dws, smalls = attention_backward(
            grad_arrived, slot_ids[t], seq_lengths[t, 0], dense_full, small, saved
        )
        returned = lax.all_to_all(
            placed_back.reshape(experts, cap, width), "exp", split_axis=0, concat_axis=1, tiled=True
        ).reshape(le, rows, width)
        input_grads.append(
            (grad_mixed + returned.astype(F32)).astype(BF).reshape(le, 1, sources, cap, width)
        )
        smalls = smalls + [
            jnp.sum(grad_normed * normal_two, axis=(0, 1)),
            jnp.sum(grad_normed, axis=(0, 1)),
        ]
        expert_parts = [jnp.stack(dwi), jnp.stack(dwo), jnp.stack(dbi), dbo]
        if t == 0:
            dense_total, small_total, expert_total = dws, smalls, expert_parts
        else:
            dense_total = [a + b for a, b in zip(dense_total, dws)]
            small_total = [a + b for a, b in zip(small_total, smalls)]
            expert_total = [a + b for a, b in zip(expert_total, expert_parts)]

    dwi, dwo, dbi, dbo = expert_total
    grad_in = dwi[:, :, :hidden] + lax.ppermute(dwi[:, :, hidden:].astype(BF), "fsdp", near).astype(F32)
    grad_out = dwo[:, :hidden] + lax.ppermute(dwo[:, hidden:].astype(BF), "fsdp", near).astype(F32)
    vectors = lax.ppermute(jnp.concatenate([dbi[:, hidden:], dbo], axis=1), "fsdp", near)
    grad_in_bias = dbi[:, :hidden] + vectors[:, :hidden]
    dbo = dbo + vectors[:, hidden:]
    grad_out_bias = lax.dynamic_slice_in_dim(dbo, fi * (width // n_f), width // n_f, 1)

    blocks = jnp.stack(
        [a.reshape(n_exp * n_f, share, width) for a in dense_total], axis=1
    ).reshape(n_exp * n_f, 4 * share, width)
    dense = reduce_dense(blocks, n_exp, n_f, ex, fi)
    dense = dense.reshape(4, share, width)
    smalls = lax.all_gather(jnp.stack(small_total)[None], everyone, axis=0, tiled=True)
    smalls = jnp.sum(smalls, axis=0)
    smalls = lax.dynamic_slice_in_dim(smalls, (ex * n_f + fi) * share, share, 1)
    return (
        jnp.stack(outputs),
        jnp.stack(input_grads),
        smalls[0],
        smalls[1],
        dense[0],
        smalls[2],
        dense[1],
        dense[2],
        smalls[3],
        dense[3],
        smalls[4],
        smalls[5],
        smalls[6],
        grad_in,
        grad_in_bias,
        grad_out,
        grad_out_bias,
    )


def solution(mesh):
    rows, dense, vec = (
        P(None, "exp", "fsdp", None, None, None),
        P(("exp", "fsdp"), None),
        P(("exp", "fsdp")),
    )
    experts = (P("exp", None, "fsdp"), P("exp", "fsdp"), P("exp", "fsdp", None), P("exp", "fsdp"))
    return jax.shard_map(
        body,
        mesh=mesh,
        in_specs=(
            rows,
            P(None, ("exp", "fsdp"), None, None),
            P(None, ("exp", "fsdp")),
            vec,
            vec,
            dense,
            vec,
            dense,
            dense,
            vec,
            dense,
            vec,
            vec,
            vec,
        )
        + experts
        + (rows,),
        out_specs=(rows, rows, vec, vec, dense, vec, dense, dense, vec, dense, vec, vec, vec) + experts,
        check_vma=False,
    )
```

```python
import functools
import math

import jax
import jax.numpy as jnp
from jax import lax
from jax.experimental import pallas as pl
from jax.experimental.pallas import tpu as pltpu
from jax.sharding import PartitionSpec as P

HEADS = 16
BF = jnp.bfloat16
F32 = jnp.float32


def dot(a, b, dims):
    return lax.dot_general(a, b, (dims, ((), ())), preferred_element_type=F32)


LIGHT = pl.CostEstimate(flops=1_000_000, bytes_accessed=100_000, transcendentals=0)
NN, NT, TN = ((1,), (0,)), ((1,), (1,)), ((0,), (0,))


def iota(shape, dim):
    return lax.broadcasted_iota(jnp.int32, shape, dim)


def chosen(condition):
    return jnp.where(condition, 1.0, 0.0).astype(BF)


def half_lanes(block, sub):
    lane = iota(block.shape, 1)
    width = block.shape[1] // 2
    inside = (lane < width) if sub == 0 else (lane >= width)
    return jnp.where(inside, block.astype(F32), 0.0).astype(BF)


def normal_of(rows):
    average = jnp.mean(rows, axis=-1, keepdims=True)
    centred = rows - average
    inverse = lax.rsqrt(jnp.mean(centred * centred, axis=-1, keepdims=True) + 1e-05)
    return centred * inverse, inverse


def fill_bias(bias, length):
    seq = bias.shape[0]
    query, key = iota((seq, seq), 0), iota((seq, seq), 1)
    bias[...] = jnp.where((key <= query) & (key < length), 0.0, -1e30)


def query_blocks(seq):
    block = 256 if seq % 256 == 0 else seq
    return [(start, block, start + block) for start in range(0, seq, block)]


def forward_kernel(
    length, column, row, arrived, w, small, placed, rows_out, q_out, k_out, v_out, att_out, lse_out, bias, normed
):
    slots, width = arrived.shape
    seq = column.shape[0]
    head = width // HEADS
    scale = head**-0.5
    fill_bias(bias, length[0, 0])
    chunk, tile = 128, 256

    @pl.loop(0, seq // chunk)
    def _(c):
        at = pl.ds(pl.multiple_of(c * chunk, chunk), chunk)
        pick = chosen(column[at, :] == iota((chunk, slots), 1))
        rows = dot(pick, arrived[...], NN)
        rows_out[at, :] = rows.astype(BF)
        normal, _ = normal_of(rows)
        normed[at, :] = (normal * small[0:1, :] + small[1:2, :]).astype(BF)

    @pl.loop(0, width // tile)
    def _(n):
        at = pl.ds(pl.multiple_of(n * tile, tile), tile)
        x = normed[...]
        q_out[:, at] = (dot(x, w[0, :, at], NN) + small[2:3, at]).astype(BF)
        k_out[:, at] = dot(x, w[1, :, at], NN).astype(BF)
        v_out[:, at] = (dot(x, w[2, :, at], NN) + small[3:4, at]).astype(BF)

    @pl.loop(0, HEADS // 2)
    def _(pair):
        at = pl.ds(pl.multiple_of(pair * 2 * head, 2 * head), 2 * head)
        k2, v2 = k_out[:, at], v_out[:, at]
        values = [half_lanes(v2, sub) for sub in (0, 1)]
        for start, size, reach in query_blocks(seq):
            q2 = q_out[start : start + size, at]
            total = None
            lse_block = lse_out[start : start + size, :]
            lane = iota(lse_block.shape, 1)
            for sub in (0, 1):
                s = dot(half_lanes(q2, sub), k2[:reach], NT) * scale + bias[start : start + size, :reach]
                top = jnp.max(s, axis=-1, keepdims=True)
                p = jnp.exp(s - top)
                l = jnp.sum(p, axis=-1, keepdims=True)
                out = dot((p * (1.0 / l)).astype(BF), values[sub][:reach], NN)
                total = out if sub == 0 else total + out
                lse_block = jnp.where(lane == 2 * pair + sub, top + jnp.log(l), lse_block)
            att_out[start : start + size, at] = total.astype(BF)
            lse_out[start : start + size, :] = lse_block

    @pl.loop(0, width // tile)
    def _(n):
        at = pl.ds(pl.multiple_of(n * tile, tile), tile)
        normed[:, at] = (dot(att_out[...], w[3, :, at], NN) + small[4:5, at]).astype(BF)

    @pl.loop(0, slots // chunk)
    def _(c):
        at = pl.ds(pl.multiple_of(c * chunk, chunk), chunk)
        put = chosen(row[...] == iota((chunk, seq), 0) + c * chunk)
        placed[at, :] = dot(put, normed[...], NN).astype(BF)


def attention_forward(arrived, slot_ids, length, w, small):
    slots, width = arrived.shape
    seq = slot_ids.shape[0]
    wide = jax.ShapeDtypeStruct((seq, width), BF)
    vm = pl.BlockSpec(memory_space=pltpu.VMEM)
    out = pl.pallas_call(
        forward_kernel,
        in_specs=[pl.BlockSpec(memory_space=pltpu.SMEM)] + [vm] * 5,
        out_specs=[vm] * 7,
        out_shape=[jax.ShapeDtypeStruct((slots, width), BF)]
        + [wide] * 5
        + [jax.ShapeDtypeStruct((seq, 128), F32)],
        scratch_shapes=[pltpu.VMEM((seq, seq), F32), pltpu.VMEM((seq, width), BF)],
        compiler_params=pltpu.CompilerParams(vmem_limit_bytes=48 << 20),
        cost_estimate=LIGHT,
    )(length.reshape(1, 1), slot_ids.reshape(seq, 1), slot_ids.reshape(1, seq), arrived, w, small)
    return out[0], tuple(out[1:])


def backward_kernel(
    groups, length, core, column, row, arrived, w, small, rows_in, q, k, v, att, lse,
    placed, *rest,
):
    keep, give, sums = rest[:4], rest[4:8], rest[8]
    bias, normed, grad_out, grad_att, dq, dk, dv, grad_normed = rest[9:]
    slots, width = arrived.shape
    seq = column.shape[0]
    head = width // HEADS
    scale = head**-0.5
    fill_bias(bias, length[0, 0])
    chunk, tile = 128, 256
    sums[...] = jnp.zeros_like(sums)

    @pl.loop(0, seq // chunk)
    def _(c):
        at = pl.ds(pl.multiple_of(c * chunk, chunk), chunk)
        pick = chosen(column[at, :] == iota((chunk, slots), 1))
        rows = dot(pick, arrived[...], NN)
        grad_out[at, :] = rows.astype(BF)
        sums[4:5, :] += jnp.sum(rows, axis=0, keepdims=True)
        normal, _ = normal_of(rows_in[at, :].astype(F32))
        normed[at, :] = (normal * small[0:1, :] + small[1:2, :]).astype(BF)

    @pl.loop(0, width // tile)
    def _(n):
        at = pl.ds(pl.multiple_of(n * tile, tile), tile)
        grad_att[:, at] = dot(grad_out[...], w[3, at, :], NT).astype(BF)

    @pl.loop(0, HEADS // 2)
    def _(pair):
        at = pl.ds(pl.multiple_of(pair * 2 * head, 2 * head), 2 * head)
        k2, v2 = k[:, at], v[:, at]
        keys = [half_lanes(k2, sub) for sub in (0, 1)]
        dks, dvs = [], []
        for start, size, reach in query_blocks(seq):
            span = slice(start, start + size)
            q2, g2, lse_block = q[span, at], grad_att[span, at], lse[span, :]
            lane = iota(lse_block.shape, 1)
            dq_total = dk_total = dv_total = None
            for sub in (0, 1):
                qs, gs = half_lanes(q2, sub), half_lanes(g2, sub)
                level = jnp.sum(jnp.where(lane == 2 * pair + sub, lse_block, 0.0), axis=-1, keepdims=True)
                s = dot(qs, k2[:reach], NT) * scale + bias[span, :reach]
                p = jnp.exp(s - level)
                dp = dot(gs, v2[:reach], NT)
                mean = jnp.sum(p * dp, axis=-1, keepdims=True)
                ds = (p * (dp - mean)).astype(BF)
                parts = (dot(ds, keys[sub][:reach], NN), dot(ds, qs, TN), dot(p.astype(BF), gs, TN))
                if sub == 0:
                    dq_total, dk_total, dv_total = parts
                else:
                    dq_total, dk_total, dv_total = (
                        dq_total + parts[0], dk_total + parts[1], dv_total + parts[2]
                    )
            dq[span, at] = (dq_total * scale).astype(BF)
            dks.append((reach, dk_total))
            dvs.append((reach, dv_total))
        for ref, pieces, factor in ((dk, dks, scale), (dv, dvs, 1.0)):
            before = 0
            for index, (reach, _) in enumerate(pieces):
                total = sum(piece[before:reach] for _, piece in pieces[index:])
                ref[before:reach, at] = (total * factor).astype(BF)
                before = reach

    for m, (left, right) in enumerate(((normed, dq), (normed, dk), (normed, dv), (att, grad_out))):
        write_dense(groups, keep[m], give[m], core, left, right)

    @pl.loop(0, width // tile)
    def _(n):
        at = pl.ds(pl.multiple_of(n * tile, tile), tile)
        grad_normed[:, at] = (
            dot(dq[...], w[0, at, :], NT) + dot(dk[...], w[1, at, :], NT) + dot(dv[...], w[2, at, :], NT)
        )

    @pl.loop(0, seq // chunk)
    def _(c):
        at = pl.ds(pl.multiple_of(c * chunk, chunk), chunk)
        normal, inverse = normal_of(rows_in[at, :].astype(F32))
        g = grad_normed[at, :]
        sums[0:1, :] += jnp.sum(g * normal, axis=0, keepdims=True)
        sums[1:2, :] += jnp.sum(g, axis=0, keepdims=True)
        sums[2:3, :] += jnp.sum(dq[at, :].astype(F32), axis=0, keepdims=True)
        sums[3:4, :] += jnp.sum(dv[at, :].astype(F32), axis=0, keepdims=True)
        u = g * small[0:1, :]
        back = inverse * (
            u - jnp.mean(u, axis=-1, keepdims=True) - normal * jnp.mean(u * normal, axis=-1, keepdims=True)
        )
        grad_out[at, :] = back.astype(BF)

    @pl.loop(0, slots // chunk)
    def _(c):
        at = pl.ds(pl.multiple_of(c * chunk, chunk), chunk)
        put = chosen(row[...] == iota((chunk, seq), 0) + c * chunk)
        placed[at, :] = dot(put, grad_out[...], NN).astype(BF)


def write_dense(groups, keep, give, core, left, right):
    width = right.shape[1]
    share = width // (2 * keep.shape[0])
    side = share * groups
    pieces = max(2 * side, 128) // side

    @pl.loop(0, width // (side * pieces))
    def _(step):
        at = pl.ds(pl.multiple_of(step * side * pieces, side * pieces), side * pieces)
        block = dot(left[:, at], right[...], TN).astype(BF).reshape(pieces, groups, share, width)
        for i in range(pieces):
            to = pl.ds((step * (pieces // 2) + i // 2) * groups, groups)

            @pl.when(core[0, 0] == i % 2)
            def _():
                keep[to] = block[i]

            @pl.when(core[0, 0] != i % 2)
            def _():
                give[to] = block[i]


def attention_backward(arrived, slot_ids, length, core, w, small, saved, owners, groups):
    slots, width = arrived.shape
    seq = slot_ids.shape[0]
    vm = pl.BlockSpec(memory_space=pltpu.VMEM)
    sm = pl.BlockSpec(memory_space=pltpu.SMEM)
    half = jax.ShapeDtypeStruct((owners // 2, width // owners, width), BF)
    out = pl.pallas_call(
        functools.partial(backward_kernel, groups),
        in_specs=[sm, sm] + [vm] * 11,
        out_specs=[vm] * 10,
        out_shape=[jax.ShapeDtypeStruct((slots, width), BF)] + [half] * 8 + [jax.ShapeDtypeStruct((8, width), F32)],
        scratch_shapes=[pltpu.VMEM((seq, seq), F32)]
        + [pltpu.VMEM((seq, width), BF)] * 6
        + [pltpu.VMEM((seq, width), F32)],
        compiler_params=pltpu.CompilerParams(vmem_limit_bytes=60 << 20),
        cost_estimate=LIGHT,
    )(
        length.reshape(1, 1), core.reshape(1, 1), slot_ids.reshape(seq, 1), slot_ids.reshape(1, seq),
        arrived, w, small, *saved,
    )
    return out[0], out[1:5], out[5:9], out[9]


def place_kernel(n_f, share, place, *refs):
    pieces, dense, table = refs[:-2], refs[-2], refs[-1]
    chips = len(pieces) // 2
    ex, fi = place[0, 0], place[0, 1]
    for c in range(2):
        for k in range(chips):
            for r in range(n_f):
                owner = jnp.bitwise_xor(ex, 2 * k + c) * n_f + jnp.bitwise_xor(fi, r)
                piece = pieces[c * chips + k]
                rows = pl.ds(pl.multiple_of(owner * share, share), share)
                for m in range(4):
                    dense[m, rows, :] = piece[r, m * share : (m + 1) * share, :]
                table[owner] = piece[r, 4 * share :, :]


def place_rows(pieces, ex, fi, share):
    n_f, lines, width = pieces[0].shape
    owners = len(pieces) * n_f
    vm = pl.BlockSpec(memory_space=pltpu.VMEM)
    return pl.pallas_call(
        functools.partial(place_kernel, n_f, share),
        in_specs=[pl.BlockSpec(memory_space=pltpu.SMEM)] + [vm] * len(pieces),
        out_specs=[vm] * 2,
        out_shape=[
            jax.ShapeDtypeStruct((4, owners * share, width), BF),
            jax.ShapeDtypeStruct((owners, lines - 4 * share, width), BF),
        ],
        compiler_params=pltpu.CompilerParams(vmem_limit_bytes=40 << 20),
        cost_estimate=LIGHT,
    )(jnp.stack([ex, fi]).astype(jnp.int32).reshape(1, 2), *pieces)


def add_dense_kernel(*refs):
    terms, vector, out = refs[:-2], refs[-2], refs[-1]
    share = terms[0].shape[1]
    for m in range(4):
        total = sum(ref[...].astype(F32) for ref in terms[m::4])
        out[:, m * share : (m + 1) * share, :] = total.astype(BF)
    out[:, 4 * share :, :] = vector[...].astype(BF)


def add_dense(terms, vector):
    count, share, width = terms[0].shape
    lines = vector.shape[1]
    block = pl.BlockSpec((2, share, width), lambda o: (o, 0, 0))
    return pl.pallas_call(
        add_dense_kernel,
        grid=(count // 2,),
        in_specs=[block] * len(terms) + [pl.BlockSpec((2, lines, width), lambda o: (o, 0, 0))],
        out_specs=pl.BlockSpec((2, 4 * share + lines, width), lambda o: (o, 0, 0)),
        out_shape=jax.ShapeDtypeStruct((count, 4 * share + lines, width), BF),
        cost_estimate=LIGHT,
    )(*terms, vector)


def add_near_kernel(a, c, got, out_in, out_out):
    out_in[0] = a[0] + jnp.transpose(got[0, 0].astype(F32))
    out_out[0] = c[0] + got[0, 1].astype(F32)


def add_near(dwi_own, dwo_own, got):
    le, width, hidden = dwi_own.shape
    tile = 256
    turned = pl.BlockSpec((1, width, tile), lambda j, c: (j, 0, c))
    plain = pl.BlockSpec((1, tile, width), lambda j, c: (j, c, 0))
    both = pl.BlockSpec((1, 2, tile, width), lambda j, c: (j, 0, c, 0))
    return pl.pallas_call(
        add_near_kernel,
        grid=(le, hidden // tile),
        in_specs=[turned, plain, both],
        out_specs=[turned, plain],
        out_shape=[jax.ShapeDtypeStruct(dwi_own.shape, F32), jax.ShapeDtypeStruct(dwo_own.shape, F32)],
        input_output_aliases={0: 0, 1: 1},
        cost_estimate=LIGHT,
    )(dwi_own, dwo_own, got)


def mixed_norm_kernel(rows, back, gain, shift, out):
    normal, _ = normal_of(rows[0].astype(F32) + back[0].astype(F32))
    out[0] = (normal * gain[...] + shift[...]).astype(BF)


def mixed_norm(rows, back, gain, shift):
    le, n, width = rows.shape
    block = pl.BlockSpec((1, 128, width), lambda j, c: (j, c, 0))
    line = pl.BlockSpec((1, width), lambda j, c: (0, 0))
    return pl.pallas_call(
        mixed_norm_kernel,
        grid=(le, n // 128),
        in_specs=[block, block, line, line],
        out_specs=block,
        out_shape=jax.ShapeDtypeStruct((le, n, width), BF),
        cost_estimate=LIGHT,
    )(rows, back, gain, shift)


def mixed_back_kernel(rows, back, gx, gx_far, cot, fill, gain, exact, low, sums):
    @pl.when((pl.program_id(0) == 0) & (pl.program_id(1) == 0))
    def _():
        sums[...] = jnp.zeros_like(sums)

    normal, inverse = normal_of(rows[0].astype(F32) + back[0].astype(F32))
    g = gx[0].astype(F32) + gx_far[0].astype(F32)
    sums[0:1, :] += jnp.sum(g * normal, axis=0, keepdims=True)
    sums[1:2, :] += jnp.sum(g, axis=0, keepdims=True)
    u = g * gain[...]
    total = cot[0].astype(F32) * fill[0] + inverse * (
        u - jnp.mean(u, axis=-1, keepdims=True) - normal * jnp.mean(u * normal, axis=-1, keepdims=True)
    )
    exact[0] = total
    low[0] = total.astype(BF)


def mixed_back(rows, back, gx, gx_far, cot, fill, gain):
    le, n, width = rows.shape
    block = pl.BlockSpec((1, 128, width), lambda j, c: (j, c, 0))
    mark = pl.BlockSpec((1, 128, 1), lambda j, c: (j, c, 0))
    return pl.pallas_call(
        mixed_back_kernel,
        grid=(le, n // 128),
        in_specs=[block] * 5 + [mark, pl.BlockSpec((1, width), lambda j, c: (0, 0))],
        out_specs=[block, block, pl.BlockSpec((8, width), lambda j, c: (0, 0))],
        out_shape=[
            jax.ShapeDtypeStruct((le, n, width), F32),
            jax.ShapeDtypeStruct((le, n, width), BF),
            jax.ShapeDtypeStruct((8, width), F32),
        ],
        cost_estimate=LIGHT,
    )(rows, back, gx, gx_far, cot, fill, gain)


def gelu_parts(v):
    a, b = 0.7978845608028654, 0.044715
    square = v * v
    t = jnp.tanh(a * v * (1.0 + b * square))
    half = 0.5 * (1.0 + t)
    slope = half + 0.5 * v * (1.0 - t * t) * (a * (1.0 + 3.0 * b * square))
    return v * half, slope


def expert_kernel(first, tiles, *refs):
    (x_own, x_far, g_own, g_far, fill_own, fill_far, wi_own, wi_near, wo_own, wo_near, bias) = refs[:11]
    before = [None] * 5 if first else refs[11:16]
    (out_own, out_far, gx_own, gx_far, dwi_own, dwo_own, dw_near, db, dbo,
     xs, gs, out_sum, gx_sum) = refs[11 if first else 16 :]
    h = pl.program_id(1)
    rows = x_own.shape[1]

    @pl.when(h == 0)
    def _():
        xs[:rows, :] = x_own[0]
        xs[rows:, :] = x_far[0]
        total = None
        for start, ref, fill in ((0, g_own, fill_own), (rows, g_far, fill_far)):
            g = ref[0].astype(F32) * fill[0]
            gs[start : start + rows, :] = g.astype(BF)
            part = jnp.sum(g, axis=0, keepdims=True)
            total = part if total is None else total + part
        dbo[0] = total if first else total + before[4][0]

    def tile_step(wi, wo, mine):
        x, g = xs[...], gs[...]
        inner = dot(x, wi, NN) + bias[0]
        act, slope = gelu_parts(inner)
        act = act.astype(BF)
        grad_inner = (dot(g, wo, NT) * slope).astype(BF)
        out = dot(act, wo, NN)
        gx = dot(grad_inner, wi, NT)
        dwi = dot(x, grad_inner, TN) if mine else dot(grad_inner, x, TN)
        dwo = dot(act, g, TN)
        column = jnp.sum(grad_inner.astype(F32), axis=0, keepdims=True)
        if mine:
            dwi_own[0] = dwi if first else dwi + before[0][0]
            dwo_own[0] = dwo if first else dwo + before[1][0]
        else:
            dw_near[0, 0] = (dwi if first else dwi + before[2][0, 0]).astype(dw_near.dtype)
            dw_near[0, 1] = (dwo if first else dwo + before[2][0, 1]).astype(dw_near.dtype)
        db[0] = column if first else column + before[3][0]

        @pl.when(h == 0)
        def _():
            out_sum[...] = out
            gx_sum[...] = gx

        @pl.when(h != 0)
        def _():
            out_sum[...] += out
            gx_sum[...] += gx

    @pl.when(h < tiles)
    def _():
        tile_step(wi_own[0], wo_own[0], True)

    @pl.when(h >= tiles)
    def _():
        tile_step(wi_near[0], wo_near[0], False)

    @pl.when(h == 2 * tiles - 1)
    def _():
        out_own[0] = out_sum[:rows, :].astype(BF)
        out_far[0] = out_sum[rows:, :].astype(BF)
        gx_own[0] = gx_sum[:rows, :].astype(BF)
        gx_far[0] = gx_sum[rows:, :].astype(BF)


def expert_step(x_own, x_far, g_own, g_far, fills, wi_own, wo_own, w_near, bias, before, tile=256):
    le, rows, width = x_own.shape
    hidden = wi_own.shape[2]
    tiles = hidden // tile
    first = before is None
    row = pl.BlockSpec((1, rows, width), lambda j, h: (j, 0, 0))
    mark = pl.BlockSpec((1, rows, 1), lambda j, h: (j, 0, 0))
    own_in = pl.BlockSpec((1, width, tile), lambda j, h: (j, 0, jnp.minimum(h, tiles - 1)))
    near_in = pl.BlockSpec((1, width, tile), lambda j, h: (j, 0, jnp.maximum(h - tiles, 0)))
    own_out = pl.BlockSpec((1, tile, width), lambda j, h: (j, jnp.minimum(h, tiles - 1), 0))
    near_out = pl.BlockSpec((1, tile, width), lambda j, h: (le + j, jnp.maximum(h - tiles, 0), 0))
    near_grads = pl.BlockSpec((1, 2, tile, width), lambda j, h: (j, 0, jnp.maximum(h - tiles, 0), 0))
    column = pl.BlockSpec((1, 1, tile), lambda j, h: (j, 0, h))
    line = pl.BlockSpec((1, 1, width), lambda j, h: (j, 0, 0))
    shapes = [jax.ShapeDtypeStruct((le, rows, width), BF)] * 4 + [
        jax.ShapeDtypeStruct((le, width, hidden), F32),
        jax.ShapeDtypeStruct((le, hidden, width), F32),
        jax.ShapeDtypeStruct((le, 2, hidden, width), F32 if first else BF),
        jax.ShapeDtypeStruct((le, 1, 2 * hidden), F32),
        jax.ShapeDtypeStruct((le, 1, width), F32),
    ]
    grads = [own_in, own_out, near_grads, column, line]
    operands = [x_own, x_far, g_own, g_far, *fills, wi_own, w_near, wo_own, w_near, bias]
    in_specs = [row] * 4 + [mark] * 2 + [own_in, near_in, own_out, near_out, column]
    if not first:
        operands += list(before)
        in_specs += grads
    return pl.pallas_call(
        functools.partial(expert_kernel, first, tiles),
        grid=(le, 2 * tiles),
        in_specs=in_specs,
        out_specs=[row] * 4 + grads,
        out_shape=shapes,
        scratch_shapes=[pltpu.VMEM((2 * rows, width), BF)] * 2 + [pltpu.VMEM((2 * rows, width), F32)] * 2,
        compiler_params=pltpu.CompilerParams(vmem_limit_bytes=60 << 20),
        cost_estimate=LIGHT,
    )(*operands)


def pick(array, index, dim):
    return lax.dynamic_index_in_dim(array, index, dim, keepdims=False)


def after(array, *others):
    return lax.optimization_barrier((array,) + others)[0]


def crossed(n, step):
    return [(i, i ^ step) for i in range(n)]


def gather_all(shard, first, n_exp, n_f, ex, fi, share):
    block, step = shard[None], 1
    while step < n_f:
        block = jnp.concatenate([block, lax.ppermute(block, "fsdp", crossed(n_f, step))])
        if step == 1:
            block = after(block, first)
        step *= 2
    pieces = [block] + [lax.ppermute(block, "exp", crossed(n_exp, 2 * k)) for k in range(1, n_exp // 2)]
    pieces += [lax.ppermute(piece, "exp", crossed(n_exp, 1)) for piece in pieces]
    return block, place_rows(pieces, ex, fi, share)


def reduce_plane(low, n_exp, chip):
    chips = n_exp // 2
    view = low.reshape(chips, -1, low.shape[1], low.shape[2])
    total = pick(view, chip, 0).astype(F32)
    for step in range(1, chips):
        block = pick(view, chip ^ step, 0)
        total = total + lax.ppermute(block, "exp", crossed(n_exp, 2 * step)).astype(F32)
    return total


def reduce_groups(total, n_f, fi):
    half = n_f // 2
    while half >= 1:
        pairs = total.reshape(2, half, *total.shape[1:])
        side = (fi // half) % 2
        got = lax.ppermute(pick(pairs, 1 - side, 0).astype(BF), "fsdp", crossed(n_f, half))
        total = pick(pairs, side, 0) + got.astype(F32)
        half //= 2
    return total[0]


def body(
    block_input,
    expert_ids,
    seq_lengths,
    attn_norm_gain,
    attn_norm_bias,
    query_matrix,
    query_offset_bias,
    key_matrix,
    value_matrix,
    value_offset_bias,
    output_matrix,
    attention_output_bias,
    ffn_norm_gain,
    ffn_norm_bias,
    expert_in,
    expert_in_bias,
    expert_out,
    expert_out_bias,
    out_cotangent,
):
    mb, le, _, sources, cap, width = block_input.shape
    n_exp, n_f = lax.axis_size("exp"), lax.axis_size("fsdp")
    ex, fi = lax.axis_index("exp"), lax.axis_index("fsdp")
    chip, core = ex // 2, ex % 2
    everyone = ("exp", "fsdp")
    owners = n_exp * n_f
    experts = le * n_exp
    slots = experts * cap
    rows = sources * cap
    hidden = expert_in.shape[2]
    seq = expert_ids.shape[2]
    far, near = crossed(n_f, 2), crossed(n_f, 1)
    share = attn_norm_gain.shape[0]

    ids = expert_ids[:, 0, :, 0]
    onehot = ids[:, :, None] == jnp.arange(experts, dtype=jnp.int32)
    counts = jnp.sum(onehot.astype(F32), axis=1)
    position = jnp.arange(seq, dtype=jnp.int32)
    same = (ids[:, :, None] == ids[:, None, :]) & (position[None, None, :] < position[None, :, None])
    slot_ids = ids * cap + jnp.sum(same.astype(jnp.int32), axis=2)
    packed = jnp.concatenate(
        [
            attn_norm_gain,
            attn_norm_bias,
            query_offset_bias,
            value_offset_bias,
            attention_output_bias,
            ffn_norm_gain,
            ffn_norm_bias,
            expert_out_bias.reshape(-1),
            expert_in_bias.reshape(-1),
            counts.astype(BF).reshape(-1),
        ]
    )
    lines = -(-packed.size // (16 * width)) * 16
    packed = jnp.pad(packed, (0, lines * width - packed.size)).reshape(lines, width)
    shipped = jnp.concatenate([query_matrix, key_matrix, value_matrix, output_matrix, packed])
    arrived_all = [
        lax.all_to_all(block_input[t, :, 0], "exp", split_axis=1, concat_axis=0, tiled=True).reshape(slots, width)
        for t in range(mb)
    ]
    ready, (dense_full, table) = gather_all(shipped, arrived_all[0], n_exp, n_f, ex, fi, share)
    table = table.reshape(owners, -1).astype(F32)
    cot = out_cotangent[:, :, 0].reshape(mb, le, rows, width)
    cot_far = lax.ppermute(after(cot, ready), "fsdp", far)
    w_near = lax.ppermute(after(jnp.concatenate([expert_in, expert_out]), ready), "fsdp", near)
    block_rows = block_input[:, :, 0].reshape(mb, le, rows, width)

    small = jnp.stack(
        [table[:, i * share : (i + 1) * share].reshape(-1) for i in range(7)] + [jnp.zeros((width,), F32)]
    )
    at = 7 * share
    table = table.reshape(n_exp, n_f, -1)
    mine = pick(table, ex, 0)
    bias_out = mine[:, at : at + expert_out_bias.size].reshape(n_f, le, -1).transpose(1, 0, 2).reshape(le, width)
    at += expert_out_bias.size
    bias_in = mine[:, at : at + le * hidden].reshape(n_f, le, hidden)
    bias_in = jnp.concatenate([pick(bias_in, fi, 0), pick(bias_in, fi ^ 1, 0)], axis=1)[:, None, :]
    at += le * hidden
    my_counts = table[:, :, at : at + counts.size].reshape(n_exp, n_f, mb, n_exp, le)
    my_counts = pick(my_counts, ex, 3)

    def fill(group):
        count = pick(my_counts, group, 1).transpose(1, 2, 0)[:, :, :, None]
        return (jnp.arange(cap, dtype=F32) < count).astype(F32).reshape(mb, le, rows, 1)

    fill_own, fill_far = fill(fi), fill(fi ^ 2)

    saved, back_rows, normed_two = [], [], []
    for t in range(mb):
        placed, kept = attention_forward(arrived_all[t], slot_ids[t], seq_lengths[t, 0], dense_full, small)
        saved.append(kept)
        back_rows.append(
            lax.all_to_all(
                placed.reshape(experts, cap, width), "exp", split_axis=0, concat_axis=1, tiled=True
            ).reshape(le, rows, width)
        )
        normed_two.append(mixed_norm(block_rows[t], back_rows[t], small[5:6], small[6:7]))
    normed_far = [lax.ppermute(normed_two[0], "fsdp", far)]
    for t in range(1, mb):
        rows_sent, cot_far = lax.optimization_barrier((normed_two[t], cot_far))
        normed_far.append(lax.ppermute(rows_sent, "fsdp", far))

    ffn, before = [], None
    for t in range(mb):
        ffn.append(
            expert_step(
                normed_two[t], normed_far[t], cot[t], cot_far[t], (fill_own[t], fill_far[t]),
                expert_in, expert_out, w_near, bias_in, before,
            )
        )
        before = ffn[t][4:]
    gx_far = [lax.ppermute(ffn[0][3], "fsdp", far)]
    for t in range(1, mb):
        gx_far.append(lax.ppermute(after(ffn[t][3], gx_far[t - 1]), "fsdp", far))
    dwi_own, dwo_own, dw_near, db, dbo = before
    dw_got = lax.ppermute(after(dw_near, gx_far[mb - 1]), "fsdp", near)
    out_far = lax.ppermute(after(jnp.stack([ffn[t][1] for t in range(mb)]), gx_far[mb - 1]), "fsdp", far)
    dbo = dbo[:, 0]
    vectors = lax.ppermute(jnp.concatenate([db[:, 0, hidden:], dbo], axis=1), "fsdp", near)

    input_grads, terms, small_total = [], [], None
    for t in range(mb):
        grad_mixed, to_send, norm_sums = mixed_back(
            block_rows[t], back_rows[t], ffn[t][2], gx_far[t], cot[t], fill_own[t], small[5:6]
        )
        grad_arrived = lax.all_to_all(
            to_send.reshape(le, sources, cap, width), "exp", split_axis=1, concat_axis=0, tiled=True
        ).reshape(slots, width)
        placed_back, keep, give, sums = attention_backward(
            grad_arrived, slot_ids[t], seq_lengths[t, 0], core, dense_full, small, saved[t], owners, n_f
        )
        returned = lax.all_to_all(
            placed_back.reshape(experts, cap, width), "exp", split_axis=0, concat_axis=1, tiled=True
        ).reshape(le, rows, width)
        input_grads.append(
            (grad_mixed + returned.astype(F32)).astype(BF).reshape(le, 1, sources, cap, width)
        )
        sums = jnp.concatenate([sums[:5], norm_sums[:2]])
        terms += list(keep) + [lax.ppermute(part, "exp", crossed(n_exp, 1)) for part in give]
        small_total = sums if t == 0 else small_total + sums

    vector = small_total.reshape(7, owners, share).transpose(1, 0, 2).reshape(owners, 7 * share)
    vector = jnp.pad(vector, ((0, 0), (0, width - 7 * share)))[:, None, :]
    vector = vector.reshape(n_exp // 2, 2, n_f, 1, width)
    vector = pick(vector, core, 1) + lax.ppermute(pick(vector, 1 - core, 1), "exp", crossed(n_exp, 1))
    vector = jnp.pad(vector.reshape(owners // 2, 1, width), ((0, 0), (0, 15), (0, 0)))
    grad_in, grad_out = add_near(dwi_own, dwo_own, dw_got)
    low, grad_in, grad_out, out_far = lax.optimization_barrier((add_dense(terms, vector), grad_in, grad_out, out_far))
    total = reduce_groups(reduce_plane(low, n_exp, chip), n_f, fi)
    dense = total[: 4 * share].reshape(4, share, width)
    smalls = total[4 * share, : 7 * share].reshape(7, share)

    outputs = []
    for t in range(mb):
        mixed = block_rows[t].astype(F32) + back_rows[t].astype(F32)
        ffn_out = ffn[t][0].astype(F32) + out_far[t].astype(F32) + bias_out[:, None, :]
        outputs.append(
            ((mixed + ffn_out) * fill_own[t]).astype(BF).reshape(le, 1, sources, cap, width)
        )
    grad_in_bias = db[:, 0, :hidden] + vectors[:, :hidden]
    grad_out_bias = lax.dynamic_slice_in_dim(
        dbo + vectors[:, hidden:], fi * (width // n_f), width // n_f, 1
    )
    return (
        jnp.stack(outputs),
        jnp.stack(input_grads),
        smalls[0],
        smalls[1],
        dense[0],
        smalls[2],
        dense[1],
        dense[2],
        smalls[3],
        dense[3],
        smalls[4],
        smalls[5],
        smalls[6],
        grad_in,
        grad_in_bias,
        grad_out,
        grad_out_bias,
    )


def solution(mesh):
    rows, dense, vec = (
        P(None, "exp", "fsdp", None, None, None),
        P(("exp", "fsdp"), None),
        P(("exp", "fsdp")),
    )
    experts = (P("exp", None, "fsdp"), P("exp", "fsdp"), P("exp", "fsdp", None), P("exp", "fsdp"))
    return jax.shard_map(
        body,
        mesh=mesh,
        in_specs=(
            rows,
            P(None, ("exp", "fsdp"), None, None),
            P(None, ("exp", "fsdp")),
            vec,
            vec,
            dense,
            vec,
            dense,
            dense,
            vec,
            dense,
            vec,
            vec,
            vec,
        )
        + experts
        + (rows,),
        out_specs=(rows, rows, vec, vec, dense, vec, dense, dense, vec, dense, vec, vec, vec) + experts,
        check_vma=False,
    )
```

```python
import functools
import math

import jax
import jax.numpy as jnp
from jax import lax
from jax.experimental import pallas as pl
from jax.experimental.pallas import tpu as pltpu
from jax.sharding import PartitionSpec as P

HEADS = 16
BF = jnp.bfloat16
F32 = jnp.float32


def dot(a, b, dims):
    return lax.dot_general(a, b, (dims, ((), ())), preferred_element_type=F32)


LIGHT = pl.CostEstimate(flops=1_000_000, bytes_accessed=100_000, transcendentals=0)
NN, NT, TN = ((1,), (0,)), ((1,), (1,)), ((0,), (0,))


def iota(shape, dim):
    return lax.broadcasted_iota(jnp.int32, shape, dim)


def chosen(condition):
    return jnp.where(condition, 1.0, 0.0).astype(BF)


def half_lanes(block, sub):
    lane = iota(block.shape, 1)
    width = block.shape[1] // 2
    inside = (lane < width) if sub == 0 else (lane >= width)
    return jnp.where(inside, block.astype(F32), 0.0).astype(BF)


def normal_of(rows):
    average = jnp.mean(rows, axis=-1, keepdims=True)
    centred = rows - average
    inverse = lax.rsqrt(jnp.mean(centred * centred, axis=-1, keepdims=True) + 1e-05)
    return centred * inverse, inverse


def fill_bias(bias, length):
    seq = bias.shape[0]
    query, key = iota((seq, seq), 0), iota((seq, seq), 1)
    bias[...] = jnp.where((key <= query) & (key < length), 0.0, -1e30)


def query_blocks(seq):
    block = 256 if seq % 256 == 0 else seq
    return [(start, block, start + block) for start in range(0, seq, block)]


def forward_kernel(
    length, column, row, arrived, w, small, placed, rows_out, q_out, k_out, v_out, att_out, lse_out, bias, normed
):
    slots, width = arrived.shape
    seq = column.shape[0]
    head = width // HEADS
    scale = head**-0.5
    fill_bias(bias, length[0, 0])
    chunk, tile = 128, 256

    @pl.loop(0, seq // chunk)
    def _(c):
        at = pl.ds(pl.multiple_of(c * chunk, chunk), chunk)
        pick = chosen(column[at, :] == iota((chunk, slots), 1))
        rows = dot(pick, arrived[...], NN)
        rows_out[at, :] = rows.astype(BF)
        normal, _ = normal_of(rows)
        normed[at, :] = (normal * small[0:1, :] + small[1:2, :]).astype(BF)

    @pl.loop(0, width // tile)
    def _(n):
        at = pl.ds(pl.multiple_of(n * tile, tile), tile)
        x = normed[...]
        q_out[:, at] = (dot(x, w[0, :, at], NN) + small[2:3, at]).astype(BF)
        k_out[:, at] = dot(x, w[1, :, at], NN).astype(BF)
        v_out[:, at] = (dot(x, w[2, :, at], NN) + small[3:4, at]).astype(BF)

    @pl.loop(0, HEADS // 2)
    def _(pair):
        at = pl.ds(pl.multiple_of(pair * 2 * head, 2 * head), 2 * head)
        k2, v2 = k_out[:, at], v_out[:, at]
        values = [half_lanes(v2, sub) for sub in (0, 1)]
        for start, size, reach in query_blocks(seq):
            q2 = q_out[start : start + size, at]
            total = None
            lse_block = lse_out[start : start + size, :]
            lane = iota(lse_block.shape, 1)
            for sub in (0, 1):
                s = dot(half_lanes(q2, sub), k2[:reach], NT) * scale + bias[start : start + size, :reach]
                top = jnp.max(s, axis=-1, keepdims=True)
                p = jnp.exp(s - top)
                l = jnp.sum(p, axis=-1, keepdims=True)
                out = dot((p * (1.0 / l)).astype(BF), values[sub][:reach], NN)
                total = out if sub == 0 else total + out
                lse_block = jnp.where(lane == 2 * pair + sub, top + jnp.log(l), lse_block)
            att_out[start : start + size, at] = total.astype(BF)
            lse_out[start : start + size, :] = lse_block

    @pl.loop(0, width // tile)
    def _(n):
        at = pl.ds(pl.multiple_of(n * tile, tile), tile)
        normed[:, at] = (dot(att_out[...], w[3, :, at], NN) + small[4:5, at]).astype(BF)

    @pl.loop(0, slots // chunk)
    def _(c):
        at = pl.ds(pl.multiple_of(c * chunk, chunk), chunk)
        put = chosen(row[...] == iota((chunk, seq), 0) + c * chunk)
        placed[at, :] = dot(put, normed[...], NN).astype(BF)


def attention_forward(arrived, slot_ids, length, w, small):
    slots, width = arrived.shape
    seq = slot_ids.shape[0]
    wide = jax.ShapeDtypeStruct((seq, width), BF)
    vm = pl.BlockSpec(memory_space=pltpu.VMEM)
    out = pl.pallas_call(
        forward_kernel,
        in_specs=[pl.BlockSpec(memory_space=pltpu.SMEM)] + [vm] * 5,
        out_specs=[vm] * 7,
        out_shape=[jax.ShapeDtypeStruct((slots, width), BF)]
        + [wide] * 5
        + [jax.ShapeDtypeStruct((seq, 128), F32)],
        scratch_shapes=[pltpu.VMEM((seq, seq), F32), pltpu.VMEM((seq, width), BF)],
        compiler_params=pltpu.CompilerParams(vmem_limit_bytes=48 << 20),
        cost_estimate=LIGHT,
    )(length.reshape(1, 1), slot_ids.reshape(seq, 1), slot_ids.reshape(1, seq), arrived, w, small)
    return out[0], tuple(out[1:])


def backward_kernel(
    groups, length, core, column, row, arrived, w, small, rows_in, q, k, v, att, lse,
    placed, *rest,
):
    keep, give, sums = rest[:4], rest[4:8], rest[8]
    bias, normed, grad_out, grad_att, dq, dk, dv, grad_normed = rest[9:]
    slots, width = arrived.shape
    seq = column.shape[0]
    head = width // HEADS
    scale = head**-0.5
    fill_bias(bias, length[0, 0])
    chunk, tile = 128, 256
    sums[...] = jnp.zeros_like(sums)

    @pl.loop(0, seq // chunk)
    def _(c):
        at = pl.ds(pl.multiple_of(c * chunk, chunk), chunk)
        pick = chosen(column[at, :] == iota((chunk, slots), 1))
        rows = dot(pick, arrived[...], NN)
        grad_out[at, :] = rows.astype(BF)
        sums[4:5, :] += jnp.sum(rows, axis=0, keepdims=True)
        normal, _ = normal_of(rows_in[at, :].astype(F32))
        normed[at, :] = (normal * small[0:1, :] + small[1:2, :]).astype(BF)

    @pl.loop(0, width // tile)
    def _(n):
        at = pl.ds(pl.multiple_of(n * tile, tile), tile)
        grad_att[:, at] = dot(grad_out[...], w[3, at, :], NT).astype(BF)

    @pl.loop(0, HEADS // 2)
    def _(pair):
        at = pl.ds(pl.multiple_of(pair * 2 * head, 2 * head), 2 * head)
        k2, v2 = k[:, at], v[:, at]
        keys = [half_lanes(k2, sub) for sub in (0, 1)]
        dks, dvs = [], []
        for start, size, reach in query_blocks(seq):
            span = slice(start, start + size)
            q2, g2, lse_block = q[span, at], grad_att[span, at], lse[span, :]
            lane = iota(lse_block.shape, 1)
            dq_total = dk_total = dv_total = None
            for sub in (0, 1):
                qs, gs = half_lanes(q2, sub), half_lanes(g2, sub)
                level = jnp.sum(jnp.where(lane == 2 * pair + sub, lse_block, 0.0), axis=-1, keepdims=True)
                s = dot(qs, k2[:reach], NT) * scale + bias[span, :reach]
                p = jnp.exp(s - level)
                dp = dot(gs, v2[:reach], NT)
                mean = jnp.sum(p * dp, axis=-1, keepdims=True)
                ds = (p * (dp - mean)).astype(BF)
                parts = (dot(ds, keys[sub][:reach], NN), dot(ds, qs, TN), dot(p.astype(BF), gs, TN))
                if sub == 0:
                    dq_total, dk_total, dv_total = parts
                else:
                    dq_total, dk_total, dv_total = (
                        dq_total + parts[0], dk_total + parts[1], dv_total + parts[2]
                    )
            dq[span, at] = (dq_total * scale).astype(BF)
            dks.append((reach, dk_total))
            dvs.append((reach, dv_total))
        for ref, pieces, factor in ((dk, dks, scale), (dv, dvs, 1.0)):
            before = 0
            for index, (reach, _) in enumerate(pieces):
                total = sum(piece[before:reach] for _, piece in pieces[index:])
                ref[before:reach, at] = (total * factor).astype(BF)
                before = reach

    for m, (left, right) in enumerate(((normed, dq), (normed, dk), (normed, dv), (att, grad_out))):
        write_dense(groups, keep[m], give[m], core, left, right)

    @pl.loop(0, width // tile)
    def _(n):
        at = pl.ds(pl.multiple_of(n * tile, tile), tile)
        grad_normed[:, at] = (
            dot(dq[...], w[0, at, :], NT) + dot(dk[...], w[1, at, :], NT) + dot(dv[...], w[2, at, :], NT)
        )

    @pl.loop(0, seq // chunk)
    def _(c):
        at = pl.ds(pl.multiple_of(c * chunk, chunk), chunk)
        normal, inverse = normal_of(rows_in[at, :].astype(F32))
        g = grad_normed[at, :]
        sums[0:1, :] += jnp.sum(g * normal, axis=0, keepdims=True)
        sums[1:2, :] += jnp.sum(g, axis=0, keepdims=True)
        sums[2:3, :] += jnp.sum(dq[at, :].astype(F32), axis=0, keepdims=True)
        sums[3:4, :] += jnp.sum(dv[at, :].astype(F32), axis=0, keepdims=True)
        u = g * small[0:1, :]
        back = inverse * (
            u - jnp.mean(u, axis=-1, keepdims=True) - normal * jnp.mean(u * normal, axis=-1, keepdims=True)
        )
        grad_out[at, :] = back.astype(BF)

    @pl.loop(0, slots // chunk)
    def _(c):
        at = pl.ds(pl.multiple_of(c * chunk, chunk), chunk)
        put = chosen(row[...] == iota((chunk, seq), 0) + c * chunk)
        placed[at, :] = dot(put, grad_out[...], NN).astype(BF)


def write_dense(groups, keep, give, core, left, right):
    width = right.shape[1]
    share = width // (2 * keep.shape[0])
    side = share * groups
    pieces = max(2 * side, 128) // side

    @pl.loop(0, width // (side * pieces))
    def _(step):
        at = pl.ds(pl.multiple_of(step * side * pieces, side * pieces), side * pieces)
        block = dot(left[:, at], right[...], TN).astype(BF).reshape(pieces, groups, share, width)
        for i in range(pieces):
            to = pl.ds((step * (pieces // 2) + i // 2) * groups, groups)

            @pl.when(core[0, 0] == i % 2)
            def _():
                keep[to] = block[i]

            @pl.when(core[0, 0] != i % 2)
            def _():
                give[to] = block[i]


def attention_backward(arrived, slot_ids, length, core, w, small, saved, owners, groups):
    slots, width = arrived.shape
    seq = slot_ids.shape[0]
    vm = pl.BlockSpec(memory_space=pltpu.VMEM)
    sm = pl.BlockSpec(memory_space=pltpu.SMEM)
    half = jax.ShapeDtypeStruct((owners // 2, width // owners, width), BF)
    out = pl.pallas_call(
        functools.partial(backward_kernel, groups),
        in_specs=[sm, sm] + [vm] * 11,
        out_specs=[vm] * 10,
        out_shape=[jax.ShapeDtypeStruct((slots, width), BF)] + [half] * 8 + [jax.ShapeDtypeStruct((8, width), F32)],
        scratch_shapes=[pltpu.VMEM((seq, seq), F32)]
        + [pltpu.VMEM((seq, width), BF)] * 6
        + [pltpu.VMEM((seq, width), F32)],
        compiler_params=pltpu.CompilerParams(vmem_limit_bytes=60 << 20),
        cost_estimate=LIGHT,
    )(
        length.reshape(1, 1), core.reshape(1, 1), slot_ids.reshape(seq, 1), slot_ids.reshape(1, seq),
        arrived, w, small, *saved,
    )
    return out[0], out[1:5], out[5:9], out[9]


def place_kernel(n_f, share, place, *refs):
    pieces, dense, table = refs[:-2], refs[-2], refs[-1]
    chips = len(pieces) // 2
    ex, fi = place[0, 0], place[0, 1]
    for c in range(2):
        for k in range(chips):
            for r in range(n_f):
                owner = jnp.bitwise_xor(ex, 2 * k + c) * n_f + jnp.bitwise_xor(fi, r)
                piece = pieces[c * chips + k]
                rows = pl.ds(pl.multiple_of(owner * share, share), share)
                for m in range(4):
                    dense[m, rows, :] = piece[r, m * share : (m + 1) * share, :]
                table[owner] = piece[r, 4 * share :, :]


def place_rows(pieces, ex, fi, share):
    n_f, lines, width = pieces[0].shape
    owners = len(pieces) * n_f
    vm = pl.BlockSpec(memory_space=pltpu.VMEM)
    return pl.pallas_call(
        functools.partial(place_kernel, n_f, share),
        in_specs=[pl.BlockSpec(memory_space=pltpu.SMEM)] + [vm] * len(pieces),
        out_specs=[vm] * 2,
        out_shape=[
            jax.ShapeDtypeStruct((4, owners * share, width), BF),
            jax.ShapeDtypeStruct((owners, lines - 4 * share, width), BF),
        ],
        compiler_params=pltpu.CompilerParams(vmem_limit_bytes=40 << 20),
        cost_estimate=LIGHT,
    )(jnp.stack([ex, fi]).astype(jnp.int32).reshape(1, 2), *pieces)


def rows_of(blocks):
    return blocks.reshape(-1, blocks.shape[-1])


def add_dense_kernel(groups, place, *refs):
    chips = refs[0].shape[0] // groups
    outs, (sums, got), terms = refs[-chips:], refs[-chips - 2 : -chips], refs[: -chips - 2]
    share = terms[0].shape[1]
    small = sums[...] + got[...]
    for k, out in enumerate(outs):
        owner = jnp.bitwise_xor(place[0, 0], k) * groups
        for f in range(groups):
            for m in range(4):
                total = sum(ref[owner + f].astype(F32) for ref in terms[m::4])
                at = (f * 4 + m) * share
                out[at : at + share, :] = total.astype(BF)
        out[groups * 4 * share :, :] = jnp.concatenate([small, jnp.zeros_like(small)]).astype(BF)


def add_dense(terms, sums, sums_got, chip, groups):
    count, share, width = terms[0].shape
    vm = pl.BlockSpec(memory_space=pltpu.VMEM)
    out = jax.ShapeDtypeStruct((groups * 4 * share + 16, width), BF)
    return pl.pallas_call(
        functools.partial(add_dense_kernel, groups),
        in_specs=[pl.BlockSpec(memory_space=pltpu.SMEM)] + [vm] * (len(terms) + 2),
        out_specs=[vm] * (count // groups),
        out_shape=[out] * (count // groups),
        compiler_params=pltpu.CompilerParams(vmem_limit_bytes=48 << 20),
        cost_estimate=LIGHT,
    )(chip.reshape(1, 1), *terms, sums, sums_got)


def add_plane_kernel(side, first, *refs):
    got, (keep, give, sums) = refs[:-3], refs[-3:]
    half = keep.shape[0]

    def total(at, n):
        at = at if isinstance(at, int) else pl.multiple_of(at, 16)
        return sum((ref[pl.ds(at, n), :].astype(F32) for ref in got), first[pl.ds(at, n), :].astype(F32))

    step = 128 if half % 128 == 0 else half
    for at in range(0, half, step):
        keep[at : at + step, :] = total(side[0, 0] * half + at, step)
        give[at : at + step, :] = total((1 - side[0, 0]) * half + at, step).astype(BF)
    small = total(2 * half, 16)
    sums[...] = small
    give[half:, :] = small.astype(BF)


def add_plane(side, first, got):
    lines, width = first.shape
    half = (lines - 16) // 2
    vm = pl.BlockSpec(memory_space=pltpu.VMEM)
    return pl.pallas_call(
        add_plane_kernel,
        in_specs=[pl.BlockSpec(memory_space=pltpu.SMEM)] + [vm] * (1 + len(got)),
        out_specs=[vm] * 3,
        out_shape=[
            jax.ShapeDtypeStruct((half, width), F32),
            jax.ShapeDtypeStruct((half + 16, width), BF),
            jax.ShapeDtypeStruct((16, width), F32),
        ],
        compiler_params=pltpu.CompilerParams(vmem_limit_bytes=48 << 20),
        cost_estimate=LIGHT,
    )(side.reshape(1, 1), first, *got)


def add_near_kernel(a, c, got, out_in, out_out):
    out_in[0] = a[0] + jnp.transpose(got[0, 0].astype(F32))
    out_out[0] = c[0] + got[0, 1].astype(F32)


def add_near(dwi_own, dwo_own, got):
    le, width, hidden = dwi_own.shape
    tile = 256
    turned = pl.BlockSpec((1, width, tile), lambda j, c: (j, 0, c))
    plain = pl.BlockSpec((1, tile, width), lambda j, c: (j, c, 0))
    both = pl.BlockSpec((1, 2, tile, width), lambda j, c: (j, 0, c, 0))
    return pl.pallas_call(
        add_near_kernel,
        grid=(le, hidden // tile),
        in_specs=[turned, plain, both],
        out_specs=[turned, plain],
        out_shape=[jax.ShapeDtypeStruct(dwi_own.shape, F32), jax.ShapeDtypeStruct(dwo_own.shape, F32)],
        input_output_aliases={0: 0, 1: 1},
        cost_estimate=LIGHT,
    )(dwi_own, dwo_own, got)


def side_of(array, place):
    return place[0] if array.shape[0] > 1 else 0


def mixed_norm_kernel(rows, back, gain, shift, out):
    normal, _ = normal_of(rows[0, 0].astype(F32) + back[0].astype(F32))
    out[0] = (normal * gain[...] + shift[...]).astype(BF)


def mixed_norm(t, rows, back, gain, shift):
    le, n, width = back.shape
    block = pl.BlockSpec((1, 128, width), lambda j, c: (j, c, 0))
    line = pl.BlockSpec((1, width), lambda j, c: (0, 0))
    return pl.pallas_call(
        mixed_norm_kernel,
        grid=(le, n // 128),
        in_specs=[pl.BlockSpec((1, 1, 128, width), lambda j, c: (t, j, c, 0)), block, line, line],
        out_specs=block,
        out_shape=jax.ShapeDtypeStruct((le, n, width), BF),
        cost_estimate=LIGHT,
    )(rows, back, gain, shift)


def mixed_back_kernel(_, rows, back, gx, gx_far, cot, fill, gain, exact, low, sums):
    @pl.when((pl.program_id(0) == 0) & (pl.program_id(1) == 0))
    def _():
        sums[...] = jnp.zeros_like(sums)

    normal, inverse = normal_of(rows[0, 0].astype(F32) + back[0].astype(F32))
    g = gx[0].astype(F32) + gx_far[0, 0].astype(F32)
    sums[0:1, :] += jnp.sum(g * normal, axis=0, keepdims=True)
    sums[1:2, :] += jnp.sum(g, axis=0, keepdims=True)
    u = g * gain[...]
    total = cot[0, 0].astype(F32) * fill[0] + inverse * (
        u - jnp.mean(u, axis=-1, keepdims=True) - normal * jnp.mean(u * normal, axis=-1, keepdims=True)
    )
    exact[0] = total
    low[0] = total.astype(BF)


def mixed_back(t, other, rows, back, gx, gx_far, cot, fill, gain):
    le, n, width = back.shape
    block = pl.BlockSpec((1, 128, width), lambda j, c, s: (j, c, 0))
    whole = pl.BlockSpec((1, 1, 128, width), lambda j, c, s: (t, j, c, 0))
    return pl.pallas_call(
        mixed_back_kernel,
        grid_spec=pltpu.PrefetchScalarGridSpec(
            num_scalar_prefetch=1,
            grid=(le, n // 128),
            in_specs=[
                whole, block, block,
                pl.BlockSpec((1, 1, 128, width), lambda j, c, s: (side_of(gx_far, s), j, c, 0)),
                whole,
                pl.BlockSpec((1, 128, 1), lambda j, c, s: (j, c, 0)),
                pl.BlockSpec((1, width), lambda j, c, s: (0, 0)),
            ],
            out_specs=[block, block, pl.BlockSpec((8, width), lambda j, c, s: (0, 0))],
        ),
        out_shape=[
            jax.ShapeDtypeStruct((le, n, width), F32),
            jax.ShapeDtypeStruct((le, n, width), BF),
            jax.ShapeDtypeStruct((8, width), F32),
        ],
        cost_estimate=LIGHT,
    )(other, rows, back, gx, gx_far, cot, fill, gain)


def gelu_parts(v):
    a, b = 0.7978845608028654, 0.044715
    square = v * v
    t = jnp.tanh(a * v * (1.0 + b * square))
    half = 0.5 * (1.0 + t)
    slope = half + 0.5 * v * (1.0 - t * t) * (a * (1.0 + 3.0 * b * square))
    return v * half, slope


def expert_kernel(first, tiles, _, *refs):
    (x_own, x_far, g_own, g_far, fill_own, fill_far, wi_own, wi_near, wo_own, wo_near, bias) = refs[:11]
    before = [None] * 5 if first else refs[11:16]
    (out_own, out_far, gx_own, gx_far, dwi_own, dwo_own, dw_near, db, dbo,
     xs, gs, out_sum, gx_sum) = refs[11 if first else 16 :]
    h = pl.program_id(1)
    rows = x_own.shape[1]

    @pl.when(h == 0)
    def _():
        xs[:rows, :] = x_own[0]
        xs[rows:, :] = x_far[0, 0]
        total = None
        for start, ref, fill in ((0, g_own[0, 0], fill_own), (rows, g_far[0, 0, 0], fill_far)):
            g = ref.astype(F32) * fill[0]
            gs[start : start + rows, :] = g.astype(BF)
            part = jnp.sum(g, axis=0, keepdims=True)
            total = part if total is None else total + part
        out_sum[...] = jnp.zeros_like(out_sum)
        gx_sum[...] = jnp.zeros_like(gx_sum)
        dbo[0] = total if first else total + before[4][0]

    def tile_step(wi, wo, mine):
        x, g = xs[...], gs[...]
        inner = dot(x, wi, NN) + bias[0]
        act, slope = gelu_parts(inner)
        act = act.astype(BF)
        grad_inner = (dot(g, wo, NT) * slope).astype(BF)
        out_sum[...] += dot(act, wo, NN)
        gx_sum[...] += dot(grad_inner, wi, NT)
        dwi = dot(x, grad_inner, TN) if mine else dot(grad_inner, x, TN)
        dwo = dot(act, g, TN)
        column = jnp.sum(grad_inner.astype(F32), axis=0, keepdims=True)
        if mine:
            dwi_own[0] = dwi if first else dwi + before[0][0]
            dwo_own[0] = dwo if first else dwo + before[1][0]
        else:
            dw_near[0, 0] = (dwi if first else dwi + before[2][0, 0].astype(F32)).astype(dw_near.dtype)
            dw_near[0, 1] = (dwo if first else dwo + before[2][0, 1].astype(F32)).astype(dw_near.dtype)
        db[0] = column if first else column + before[3][0]

    @pl.when(h < tiles)
    def _():
        tile_step(wi_own[0], wo_own[0], True)

    @pl.when(h >= tiles)
    def _():
        tile_step(wi_near[0], wo_near[0], False)

    @pl.when(h == 2 * tiles - 1)
    def _():
        out_own[0] = out_sum[:rows, :].astype(BF)
        out_far[0] = out_sum[rows:, :].astype(BF)
        gx_own[0] = gx_sum[:rows, :].astype(BF)
        gx_far[0] = gx_sum[rows:, :].astype(BF)


def expert_step(t, other, x_own, x_far, g_own, g_far, fills, wi_own, wo_own, w_near, bias, before, tile=512):
    le, rows, width = x_own.shape
    hidden = wi_own.shape[2]
    tiles = hidden // tile
    first = before is None
    mode = None if first else pl.Buffered(1)
    out_row = pl.BlockSpec((1, rows, width), lambda j, h, s: (j, 0, 0))
    mark = pl.BlockSpec((1, rows, 1), lambda j, h, s: (j, 0, 0), pipeline_mode=mode)
    own = lambda h: jnp.minimum(h, tiles - 1)
    near = lambda h: jnp.maximum(h - tiles, 0)
    shapes = [jax.ShapeDtypeStruct((le, rows, width), BF)] * 4 + [
        jax.ShapeDtypeStruct((le, width, hidden), F32),
        jax.ShapeDtypeStruct((le, hidden, width), F32),
        jax.ShapeDtypeStruct((le, 2, hidden, width), BF),
        jax.ShapeDtypeStruct((le, 1, 2 * hidden), F32),
        jax.ShapeDtypeStruct((le, 1, width), F32),
    ]
    own_in = pl.BlockSpec((1, width, tile), lambda j, h, s: (j, 0, own(h)))
    own_out = pl.BlockSpec((1, tile, width), lambda j, h, s: (j, own(h), 0))
    column = pl.BlockSpec((1, 1, tile), lambda j, h, s: (j, 0, h))
    grads = [
        own_in,
        own_out,
        pl.BlockSpec((1, 2, tile, width), lambda j, h, s: (j, 0, near(h), 0)),
        column,
        pl.BlockSpec((1, 1, width), lambda j, h, s: (j, 0, 0)),
    ]
    operands = [x_own, x_far, g_own, g_far, *fills, wi_own, w_near, wo_own, w_near, bias]
    in_specs = [
        pl.BlockSpec((1, rows, width), lambda j, h, s: (j, 0, 0), pipeline_mode=mode),
        pl.BlockSpec((1, 1, rows, width), lambda j, h, s: (side_of(x_far, s), j, 0, 0), pipeline_mode=mode),
        pl.BlockSpec((1, 1, rows, width), lambda j, h, s: (t, j, 0, 0), pipeline_mode=mode),
        pl.BlockSpec((1, 1, 1, rows, width), lambda j, h, s: (side_of(g_far, s), t, j, 0, 0), pipeline_mode=mode),
        mark,
        mark,
        own_in,
        pl.BlockSpec((1, width, tile), lambda j, h, s: (j, 0, near(h))),
        own_out,
        pl.BlockSpec((1, tile, width), lambda j, h, s: (le + j, near(h), 0)),
        column,
    ]
    if not first:
        operands += list(before)
        near_before = pl.BlockSpec((1, 2, tile, width), lambda j, h, s: (j, 0, near(h), 0), pipeline_mode=mode)
        in_specs += grads[:2] + [near_before] + grads[3:]
    return pl.pallas_call(
        functools.partial(expert_kernel, first, tiles),
        grid_spec=pltpu.PrefetchScalarGridSpec(
            num_scalar_prefetch=1,
            grid=(le, 2 * tiles),
            in_specs=in_specs,
            out_specs=[out_row] * 4 + grads,
            scratch_shapes=[pltpu.VMEM((2 * rows, width), BF)] * 2 + [pltpu.VMEM((2 * rows, width), F32)] * 2,
        ),
        out_shape=shapes,
        compiler_params=pltpu.CompilerParams(vmem_limit_bytes=60 << 20),
        cost_estimate=LIGHT,
    )(other, *operands)


def pick(array, index, dim):
    return lax.dynamic_index_in_dim(array, index, dim, keepdims=False)


def after(array, *others):
    return lax.optimization_barrier((array,) + others)[0]


def crossed(n, step):
    return [(i, i ^ step) for i in range(n)]


def both_groups(array, n_f):
    pairs = [[i, i ^ 2] for i in range(n_f) if not i & 2]
    return lax.all_gather(array, "fsdp", axis_index_groups=pairs)


def gather_all(shard, first, n_exp, n_f, ex, fi, share):
    block, step = shard[None], 1
    while step < n_f:
        block = jnp.concatenate([block, lax.ppermute(block, "fsdp", crossed(n_f, step))])
        if step == 1:
            block = after(block, first)
        step *= 2
    pieces = [block] + [lax.ppermute(block, "exp", crossed(n_exp, 2 * k)) for k in range(1, n_exp // 2)]
    pieces += [lax.ppermute(piece, "exp", crossed(n_exp, 1)) for piece in pieces]
    return block, place_rows(pieces, ex, fi, share)


def body(
    block_input,
    expert_ids,
    seq_lengths,
    attn_norm_gain,
    attn_norm_bias,
    query_matrix,
    query_offset_bias,
    key_matrix,
    value_matrix,
    value_offset_bias,
    output_matrix,
    attention_output_bias,
    ffn_norm_gain,
    ffn_norm_bias,
    expert_in,
    expert_in_bias,
    expert_out,
    expert_out_bias,
    out_cotangent,
):
    mb, le, _, sources, cap, width = block_input.shape
    n_exp, n_f = lax.axis_size("exp"), lax.axis_size("fsdp")
    ex, fi = lax.axis_index("exp"), lax.axis_index("fsdp")
    chip, core = ex // 2, ex % 2
    everyone = ("exp", "fsdp")
    owners = n_exp * n_f
    experts = le * n_exp
    slots = experts * cap
    rows = sources * cap
    hidden = expert_in.shape[2]
    seq = expert_ids.shape[2]
    far, near = crossed(n_f, 2), crossed(n_f, 1)
    share = attn_norm_gain.shape[0]

    ids = expert_ids[:, 0, :, 0]
    onehot = ids[:, :, None] == jnp.arange(experts, dtype=jnp.int32)
    counts = jnp.sum(onehot.astype(F32), axis=1)
    position = jnp.arange(seq, dtype=jnp.int32)
    same = (ids[:, :, None] == ids[:, None, :]) & (position[None, None, :] < position[None, :, None])
    slot_ids = ids * cap + jnp.sum(same.astype(jnp.int32), axis=2)
    packed = jnp.concatenate(
        [
            attn_norm_gain,
            attn_norm_bias,
            query_offset_bias,
            value_offset_bias,
            attention_output_bias,
            ffn_norm_gain,
            ffn_norm_bias,
            expert_out_bias.reshape(-1),
            expert_in_bias.reshape(-1),
            counts.astype(BF).reshape(-1),
        ]
    )
    lines = -(-packed.size // (16 * width)) * 16
    packed = jnp.pad(packed, (0, lines * width - packed.size)).reshape(lines, width)
    shipped = jnp.concatenate([query_matrix, key_matrix, value_matrix, output_matrix, packed])
    arrived_all = [
        lax.all_to_all(block_input[t, :, 0], "exp", split_axis=1, concat_axis=0, tiled=True).reshape(slots, width)
        for t in range(mb)
    ]
    ready, (dense_full, table) = gather_all(shipped, arrived_all[0], n_exp, n_f, ex, fi, share)
    table = table.reshape(owners, -1).astype(F32)
    cot = out_cotangent[:, :, 0].reshape(mb, le, rows, width)
    other = (1 - (fi // 2) % 2).astype(jnp.int32).reshape(1)
    cot_far = both_groups(after(cot, ready), n_f)
    w_near = lax.ppermute(after(jnp.concatenate([expert_in, expert_out]), ready), "fsdp", near)
    block_rows = block_input[:, :, 0].reshape(mb, le, rows, width)

    small = jnp.stack(
        [table[:, i * share : (i + 1) * share].reshape(-1) for i in range(7)] + [jnp.zeros((width,), F32)]
    )
    at = 7 * share
    table = table.reshape(n_exp, n_f, -1)
    mine = pick(table, ex, 0)
    bias_out = mine[:, at : at + expert_out_bias.size].reshape(n_f, le, -1).transpose(1, 0, 2).reshape(le, width)
    at += expert_out_bias.size
    bias_in = mine[:, at : at + le * hidden].reshape(n_f, le, hidden)
    bias_in = jnp.concatenate([pick(bias_in, fi, 0), pick(bias_in, fi ^ 1, 0)], axis=1)[:, None, :]
    at += le * hidden
    my_counts = table[:, :, at : at + counts.size].reshape(n_exp, n_f, mb, n_exp, le)
    my_counts = pick(my_counts, ex, 3)

    def fill(group):
        count = pick(my_counts, group, 1).transpose(1, 2, 0)[:, :, :, None]
        return (jnp.arange(cap, dtype=F32) < count).astype(F32).reshape(mb, le, rows, 1)

    fill_own, fill_far = fill(fi), fill(fi ^ 2)

    saved, back_rows, normed_two = [], [], []
    for t in range(mb):
        placed, kept = attention_forward(arrived_all[t], slot_ids[t], seq_lengths[t, 0], dense_full, small)
        saved.append(kept)
        back_rows.append(
            lax.all_to_all(
                placed.reshape(experts, cap, width), "exp", split_axis=0, concat_axis=1, tiled=True
            ).reshape(le, rows, width)
        )
        normed_two.append(mixed_norm(t, block_rows, back_rows[t], small[5:6], small[6:7]))
    normed_far = [lax.ppermute(normed_two[0], "fsdp", far)[None]]
    for t in range(1, mb):
        rows_sent, cot_far = lax.optimization_barrier((normed_two[t], cot_far))
        normed_far.append(lax.ppermute(rows_sent, "fsdp", far)[None])

    ffn, before = [], None
    for t in range(mb):
        ffn.append(
            expert_step(
                t, other, normed_two[t], normed_far[t], cot, cot_far, (fill_own[t], fill_far[t]),
                expert_in, expert_out, w_near, bias_in, before,
            )
        )
        before = ffn[t][4:]
    gx_far = [lax.ppermute(ffn[0][3], "fsdp", far)[None]]
    for t in range(1, mb):
        gx_far.append(both_groups(after(ffn[t][3], gx_far[t - 1]), n_f))
    dwi_own, dwo_own, dw_near, db, dbo = before
    dbo = dbo[:, 0]
    vectors = jnp.concatenate([db[:, 0, hidden:], dbo], axis=1)

    dw_got = lax.ppermute(dw_near, "fsdp", near)
    input_grads, terms, small_total = [], [], None
    for t in range(mb):
        got = gx_far[t]
        if t == mb - 1:
            outs = jnp.stack([ffn[i][1] for i in range(mb)])
            got, outs, placed_back = lax.optimization_barrier((got, outs, placed_back))
            out_far = both_groups(outs, n_f)
        grad_mixed, to_send, norm_sums = mixed_back(
            t, other, block_rows, back_rows[t], ffn[t][2], got, cot, fill_own[t], small[5:6]
        )
        grad_arrived = lax.all_to_all(
            to_send.reshape(le, sources, cap, width), "exp", split_axis=1, concat_axis=0, tiled=True
        ).reshape(slots, width)
        placed_back, keep, give, sums = attention_backward(
            grad_arrived, slot_ids[t], seq_lengths[t, 0], core, dense_full, small, saved[t], owners, n_f
        )
        returned = lax.all_to_all(
            placed_back.reshape(experts, cap, width), "exp", split_axis=0, concat_axis=1, tiled=True
        ).reshape(le, rows, width)
        input_grads.append(
            (grad_mixed + returned.astype(F32)).astype(BF).reshape(le, 1, sources, cap, width)
        )
        sums = jnp.concatenate([sums[:5], norm_sums[:2], norm_sums[7:]])
        terms += list(keep) + [lax.ppermute(part, "exp", crossed(n_exp, 1)) for part in give]
        small_total = sums if t == 0 else small_total + sums

    sums_got = lax.ppermute(small_total, "exp", crossed(n_exp, 1))
    blocks = add_dense(terms, small_total, sums_got, chip, n_f)
    got = [lax.ppermute(blocks[k], "exp", crossed(n_exp, 2 * k)) for k in range(1, n_exp // 2)]
    keep, give, sums = add_plane((fi // 2) % 2, blocks[0], got)
    far_got = lax.ppermute(give, "fsdp", far)
    outputs = []
    far_outs = pick(out_far, other[0], 0)
    for t in range(mb):
        mixed = block_rows[t].astype(F32) + back_rows[t].astype(F32)
        ffn_out = ffn[t][0].astype(F32) + far_outs[t].astype(F32) + bias_out[:, None, :]
        outputs.append(
            ((mixed + ffn_out) * fill_own[t]).astype(BF).reshape(le, 1, sources, cap, width)
        )
    outputs = jnp.stack(outputs)
    half = keep.shape[0]
    keep = keep + far_got[:half].astype(F32)
    sums = sums + far_got[half:].astype(F32)
    pairs = keep.reshape(2, 4 * share, width)
    ride = jnp.pad(vectors, ((0, 0), (0, -vectors.shape[1] % width))).reshape(-1, width)
    give = jnp.concatenate([pick(pairs, 1 - fi % 2, 0), sums, ride]).astype(BF)
    give, outputs = lax.optimization_barrier((give, outputs))
    near_got = lax.ppermute(give, "fsdp", near).astype(F32)
    total = pick(pairs, fi % 2, 0) + near_got[: 4 * share]
    sums = sums + near_got[4 * share : 4 * share + 16]
    vectors_got = near_got[4 * share + 16 :].reshape(le, -1)[:, : vectors.shape[1]]
    grad_in, grad_out = add_near(dwi_own, dwo_own, dw_got)
    dense = total.reshape(4, share, width)
    smalls = lax.dynamic_slice_in_dim(sums, (ex * n_f + fi) * share, share, 1)

    grad_in_bias = db[:, 0, :hidden] + vectors_got[:, :hidden]
    grad_out_bias = lax.dynamic_slice_in_dim(
        dbo + vectors_got[:, hidden:], fi * (width // n_f), width // n_f, 1
    )
    return (
        outputs,
        jnp.stack(input_grads),
        smalls[0],
        smalls[1],
        dense[0],
        smalls[2],
        dense[1],
        dense[2],
        smalls[3],
        dense[3],
        smalls[4],
        smalls[5],
        smalls[6],
        grad_in,
        grad_in_bias,
        grad_out,
        grad_out_bias,
    )


def solution(mesh):
    rows, dense, vec = (
        P(None, "exp", "fsdp", None, None, None),
        P(("exp", "fsdp"), None),
        P(("exp", "fsdp")),
    )
    experts = (P("exp", None, "fsdp"), P("exp", "fsdp"), P("exp", "fsdp", None), P("exp", "fsdp"))
    return jax.shard_map(
        body,
        mesh=mesh,
        in_specs=(
            rows,
            P(None, ("exp", "fsdp"), None, None),
            P(None, ("exp", "fsdp")),
            vec,
            vec,
            dense,
            vec,
            dense,
            dense,
            vec,
            dense,
            vec,
            vec,
            vec,
        )
        + experts
        + (rows,),
        out_specs=(rows, rows, vec, vec, dense, vec, dense, dense, vec, dense, vec, vec, vec) + experts,
        check_vma=False,
    )
```

```python
import functools
import math

import jax
import jax.numpy as jnp
from jax import lax
from jax.experimental import pallas as pl
from jax.experimental.pallas import tpu as pltpu
from jax.sharding import PartitionSpec as P

HEADS = 16
BF = jnp.bfloat16
F32 = jnp.float32


def dot(a, b, dims):
    return lax.dot_general(a, b, (dims, ((), ())), preferred_element_type=F32)


LIGHT = pl.CostEstimate(flops=1_000_000, bytes_accessed=100_000, transcendentals=0)
NN, NT, TN = ((1,), (0,)), ((1,), (1,)), ((0,), (0,))


def iota(shape, dim):
    return lax.broadcasted_iota(jnp.int32, shape, dim)


def chosen(condition):
    return jnp.where(condition, 1.0, 0.0).astype(BF)


def half_lanes(block, sub):
    lane = iota(block.shape, 1)
    width = block.shape[1] // 2
    inside = (lane < width) if sub == 0 else (lane >= width)
    return jnp.where(inside, block.astype(F32), 0.0).astype(BF)


def normal_of(rows):
    average = jnp.mean(rows, axis=-1, keepdims=True)
    centred = rows - average
    inverse = lax.rsqrt(jnp.mean(centred * centred, axis=-1, keepdims=True) + 1e-05)
    return centred * inverse, inverse


def fill_bias(bias, length):
    seq = bias.shape[0]
    query, key = iota((seq, seq), 0), iota((seq, seq), 1)
    bias[...] = jnp.where((key <= query) & (key < length), 0.0, -1e30)


def query_blocks(seq):
    block = 256 if seq % 256 == 0 else seq
    return [(start, block, start + block) for start in range(0, seq, block)]


def forward_kernel(
    length, column, row, arrived, w, small, placed, rows_out, q_out, k_out, v_out, att_out, lse_out, bias, normed
):
    slots, width = arrived.shape
    seq = column.shape[0]
    head = width // HEADS
    scale = head**-0.5
    fill_bias(bias, length[0, 0])
    chunk, tile = 128, 256

    @pl.loop(0, seq // chunk)
    def _(c):
        at = pl.ds(pl.multiple_of(c * chunk, chunk), chunk)
        pick = chosen(column[at, :] == iota((chunk, slots), 1))
        rows = dot(pick, arrived[...], NN)
        rows_out[at, :] = rows.astype(BF)
        normal, _ = normal_of(rows)
        normed[at, :] = (normal * small[0:1, :] + small[1:2, :]).astype(BF)

    @pl.loop(0, width // tile)
    def _(n):
        at = pl.ds(pl.multiple_of(n * tile, tile), tile)
        x = normed[...]
        q_out[:, at] = (dot(x, w[0, :, at], NN) + small[2:3, at]).astype(BF)
        k_out[:, at] = dot(x, w[1, :, at], NN).astype(BF)
        v_out[:, at] = (dot(x, w[2, :, at], NN) + small[3:4, at]).astype(BF)

    @pl.loop(0, HEADS // 2)
    def _(pair):
        at = pl.ds(pl.multiple_of(pair * 2 * head, 2 * head), 2 * head)
        k2, v2 = k_out[:, at], v_out[:, at]
        values = [half_lanes(v2, sub) for sub in (0, 1)]
        for start, size, reach in query_blocks(seq):
            q2 = q_out[start : start + size, at]
            total = None
            lse_block = lse_out[start : start + size, :]
            lane = iota(lse_block.shape, 1)
            for sub in (0, 1):
                s = dot(half_lanes(q2, sub), k2[:reach], NT) * scale + bias[start : start + size, :reach]
                top = jnp.max(s, axis=-1, keepdims=True)
                p = jnp.exp(s - top)
                l = jnp.sum(p, axis=-1, keepdims=True)
                out = dot((p * (1.0 / l)).astype(BF), values[sub][:reach], NN)
                total = out if sub == 0 else total + out
                lse_block = jnp.where(lane == 2 * pair + sub, top + jnp.log(l), lse_block)
            att_out[start : start + size, at] = total.astype(BF)
            lse_out[start : start + size, :] = lse_block

    @pl.loop(0, width // tile)
    def _(n):
        at = pl.ds(pl.multiple_of(n * tile, tile), tile)
        normed[:, at] = (dot(att_out[...], w[3, :, at], NN) + small[4:5, at]).astype(BF)

    @pl.loop(0, slots // chunk)
    def _(c):
        at = pl.ds(pl.multiple_of(c * chunk, chunk), chunk)
        put = chosen(row[...] == iota((chunk, seq), 0) + c * chunk)
        placed[at, :] = dot(put, normed[...], NN).astype(BF)


def attention_forward(arrived, slot_ids, length, w, small):
    slots, width = arrived.shape
    seq = slot_ids.shape[0]
    wide = jax.ShapeDtypeStruct((seq, width), BF)
    vm = pl.BlockSpec(memory_space=pltpu.VMEM)
    out = pl.pallas_call(
        forward_kernel,
        in_specs=[pl.BlockSpec(memory_space=pltpu.SMEM)] + [vm] * 5,
        out_specs=[vm] * 7,
        out_shape=[jax.ShapeDtypeStruct((slots, width), BF)]
        + [wide] * 5
        + [jax.ShapeDtypeStruct((seq, 128), F32)],
        scratch_shapes=[pltpu.VMEM((seq, seq), F32), pltpu.VMEM((seq, width), BF)],
        compiler_params=pltpu.CompilerParams(vmem_limit_bytes=48 << 20),
        cost_estimate=LIGHT,
    )(length.reshape(1, 1), slot_ids.reshape(seq, 1), slot_ids.reshape(1, seq), arrived, w, small)
    return out[0], tuple(out[1:])


def backward_kernel(
    groups, length, core, column, row, arrived, w, small, rows_in, q, k, v, att, lse,
    placed, *rest,
):
    keep, give, sums = rest[:4], rest[4:8], rest[8]
    bias, normed, grad_out, grad_att, dq, dk, dv, grad_normed = rest[9:]
    slots, width = arrived.shape
    seq = column.shape[0]
    head = width // HEADS
    scale = head**-0.5
    fill_bias(bias, length[0, 0])
    chunk, tile = 128, 256
    sums[...] = jnp.zeros_like(sums)

    @pl.loop(0, seq // chunk)
    def _(c):
        at = pl.ds(pl.multiple_of(c * chunk, chunk), chunk)
        pick = chosen(column[at, :] == iota((chunk, slots), 1))
        rows = dot(pick, arrived[...], NN)
        grad_out[at, :] = rows.astype(BF)
        sums[4:5, :] += jnp.sum(rows, axis=0, keepdims=True)
        normal, _ = normal_of(rows_in[at, :].astype(F32))
        normed[at, :] = (normal * small[0:1, :] + small[1:2, :]).astype(BF)

    @pl.loop(0, width // tile)
    def _(n):
        at = pl.ds(pl.multiple_of(n * tile, tile), tile)
        grad_att[:, at] = dot(grad_out[...], w[3, at, :], NT).astype(BF)

    @pl.loop(0, HEADS // 2)
    def _(pair):
        at = pl.ds(pl.multiple_of(pair * 2 * head, 2 * head), 2 * head)
        k2, v2 = k[:, at], v[:, at]
        keys = [half_lanes(k2, sub) for sub in (0, 1)]
        dks, dvs = [], []
        for start, size, reach in query_blocks(seq):
            span = slice(start, start + size)
            q2, g2, lse_block = q[span, at], grad_att[span, at], lse[span, :]
            lane = iota(lse_block.shape, 1)
            dq_total = dk_total = dv_total = None
            for sub in (0, 1):
                qs, gs = half_lanes(q2, sub), half_lanes(g2, sub)
                level = jnp.sum(jnp.where(lane == 2 * pair + sub, lse_block, 0.0), axis=-1, keepdims=True)
                s = dot(qs, k2[:reach], NT) * scale + bias[span, :reach]
                p = jnp.exp(s - level)
                dp = dot(gs, v2[:reach], NT)
                mean = jnp.sum(p * dp, axis=-1, keepdims=True)
                ds = (p * (dp - mean)).astype(BF)
                parts = (dot(ds, keys[sub][:reach], NN), dot(ds, qs, TN), dot(p.astype(BF), gs, TN))
                if sub == 0:
                    dq_total, dk_total, dv_total = parts
                else:
                    dq_total, dk_total, dv_total = (
                        dq_total + parts[0], dk_total + parts[1], dv_total + parts[2]
                    )
            dq[span, at] = (dq_total * scale).astype(BF)
            dks.append((reach, dk_total))
            dvs.append((reach, dv_total))
        for ref, pieces, factor in ((dk, dks, scale), (dv, dvs, 1.0)):
            before = 0
            for index, (reach, _) in enumerate(pieces):
                total = sum(piece[before:reach] for _, piece in pieces[index:])
                ref[before:reach, at] = (total * factor).astype(BF)
                before = reach

    for m, (left, right) in enumerate(((normed, dq), (normed, dk), (normed, dv), (att, grad_out))):
        write_dense(groups, keep[m], give[m], core, left, right)

    @pl.loop(0, width // tile)
    def _(n):
        at = pl.ds(pl.multiple_of(n * tile, tile), tile)
        grad_normed[:, at] = (
            dot(dq[...], w[0, at, :], NT) + dot(dk[...], w[1, at, :], NT) + dot(dv[...], w[2, at, :], NT)
        )

    @pl.loop(0, seq // chunk)
    def _(c):
        at = pl.ds(pl.multiple_of(c * chunk, chunk), chunk)
        normal, inverse = normal_of(rows_in[at, :].astype(F32))
        g = grad_normed[at, :]
        sums[0:1, :] += jnp.sum(g * normal, axis=0, keepdims=True)
        sums[1:2, :] += jnp.sum(g, axis=0, keepdims=True)
        sums[2:3, :] += jnp.sum(dq[at, :].astype(F32), axis=0, keepdims=True)
        sums[3:4, :] += jnp.sum(dv[at, :].astype(F32), axis=0, keepdims=True)
        u = g * small[0:1, :]
        back = inverse * (
            u - jnp.mean(u, axis=-1, keepdims=True) - normal * jnp.mean(u * normal, axis=-1, keepdims=True)
        )
        grad_out[at, :] = back.astype(BF)

    @pl.loop(0, slots // chunk)
    def _(c):
        at = pl.ds(pl.multiple_of(c * chunk, chunk), chunk)
        put = chosen(row[...] == iota((chunk, seq), 0) + c * chunk)
        placed[at, :] = dot(put, grad_out[...], NN).astype(BF)


def write_dense(groups, keep, give, core, left, right):
    width = right.shape[1]
    share = width // (2 * keep.shape[0])
    side = share * groups
    pieces = max(2 * side, 128) // side

    @pl.loop(0, width // (side * pieces))
    def _(step):
        at = pl.ds(pl.multiple_of(step * side * pieces, side * pieces), side * pieces)
        block = dot(left[:, at], right[...], TN).astype(BF).reshape(pieces, groups, share, width)
        for i in range(pieces):
            to = pl.ds((step * (pieces // 2) + i // 2) * groups, groups)

            @pl.when(core[0, 0] == i % 2)
            def _():
                keep[to] = block[i]

            @pl.when(core[0, 0] != i % 2)
            def _():
                give[to] = block[i]


def attention_backward(arrived, slot_ids, length, core, w, small, saved, owners, groups):
    slots, width = arrived.shape
    seq = slot_ids.shape[0]
    vm = pl.BlockSpec(memory_space=pltpu.VMEM)
    sm = pl.BlockSpec(memory_space=pltpu.SMEM)
    half = jax.ShapeDtypeStruct((owners // 2, width // owners, width), BF)
    out = pl.pallas_call(
        functools.partial(backward_kernel, groups),
        in_specs=[sm, sm] + [vm] * 11,
        out_specs=[vm] * 10,
        out_shape=[jax.ShapeDtypeStruct((slots, width), BF)] + [half] * 8 + [jax.ShapeDtypeStruct((8, width), F32)],
        scratch_shapes=[pltpu.VMEM((seq, seq), F32)]
        + [pltpu.VMEM((seq, width), BF)] * 6
        + [pltpu.VMEM((seq, width), F32)],
        compiler_params=pltpu.CompilerParams(vmem_limit_bytes=60 << 20),
        cost_estimate=LIGHT,
    )(
        length.reshape(1, 1), core.reshape(1, 1), slot_ids.reshape(seq, 1), slot_ids.reshape(1, seq),
        arrived, w, small, *saved,
    )
    return out[0], out[1:5], out[5:9], out[9]


def place_kernel(n_f, share, place, *refs):
    pieces, dense, table = refs[:-2], refs[-2], refs[-1]
    chips = len(pieces) // 2
    ex, fi = place[0, 0], place[0, 1]
    for c in range(2):
        for k in range(chips):
            for r in range(n_f):
                owner = jnp.bitwise_xor(ex, 2 * k + c) * n_f + jnp.bitwise_xor(fi, r)
                piece = pieces[c * chips + k]
                rows = pl.ds(pl.multiple_of(owner * share, share), share)
                for m in range(4):
                    dense[m, rows, :] = piece[r, m * share : (m + 1) * share, :]
                table[owner] = piece[r, 4 * share :, :]


def place_rows(pieces, ex, fi, share):
    n_f, lines, width = pieces[0].shape
    owners = len(pieces) * n_f
    vm = pl.BlockSpec(memory_space=pltpu.VMEM)
    return pl.pallas_call(
        functools.partial(place_kernel, n_f, share),
        in_specs=[pl.BlockSpec(memory_space=pltpu.SMEM)] + [vm] * len(pieces),
        out_specs=[vm] * 2,
        out_shape=[
            jax.ShapeDtypeStruct((4, owners * share, width), BF),
            jax.ShapeDtypeStruct((owners, lines - 4 * share, width), BF),
        ],
        compiler_params=pltpu.CompilerParams(vmem_limit_bytes=40 << 20),
        cost_estimate=LIGHT,
    )(jnp.stack([ex, fi]).astype(jnp.int32).reshape(1, 2), *pieces)


def rows_of(blocks):
    return blocks.reshape(-1, blocks.shape[-1])


def add_dense_kernel(groups, place, *refs):
    chips = refs[0].shape[0] // groups
    outs, (sums, got), terms = refs[-chips:], refs[-chips - 2 : -chips], refs[: -chips - 2]
    share = terms[0].shape[1]
    small = sums[...] + got[...]
    for k, out in enumerate(outs):
        owner = jnp.bitwise_xor(place[0, 0], k) * groups
        for f in range(groups):
            for m in range(4):
                total = sum(ref[owner + f].astype(F32) for ref in terms[m::4])
                at = (f * 4 + m) * share
                out[at : at + share, :] = total.astype(BF)
        out[groups * 4 * share :, :] = jnp.concatenate([small, jnp.zeros_like(small)]).astype(BF)


def add_dense(terms, sums, sums_got, chip, groups):
    count, share, width = terms[0].shape
    vm = pl.BlockSpec(memory_space=pltpu.VMEM)
    out = jax.ShapeDtypeStruct((groups * 4 * share + 16, width), BF)
    return pl.pallas_call(
        functools.partial(add_dense_kernel, groups),
        in_specs=[pl.BlockSpec(memory_space=pltpu.SMEM)] + [vm] * (len(terms) + 2),
        out_specs=[vm] * (count // groups),
        out_shape=[out] * (count // groups),
        compiler_params=pltpu.CompilerParams(vmem_limit_bytes=48 << 20),
        cost_estimate=LIGHT,
    )(chip.reshape(1, 1), *terms, sums, sums_got)


def add_plane_kernel(side, first, *refs):
    got, (keep, give, sums) = refs[:-3], refs[-3:]
    half = keep.shape[0]

    def total(at, n):
        at = at if isinstance(at, int) else pl.multiple_of(at, 16)
        return sum((ref[pl.ds(at, n), :].astype(F32) for ref in got), first[pl.ds(at, n), :].astype(F32))

    step = 128 if half % 128 == 0 else half
    for at in range(0, half, step):
        keep[at : at + step, :] = total(side[0, 0] * half + at, step)
        give[at : at + step, :] = total((1 - side[0, 0]) * half + at, step).astype(BF)
    small = total(2 * half, 16)
    sums[...] = small
    give[half:, :] = small.astype(BF)


def add_plane(side, first, got):
    lines, width = first.shape
    half = (lines - 16) // 2
    vm = pl.BlockSpec(memory_space=pltpu.VMEM)
    return pl.pallas_call(
        add_plane_kernel,
        in_specs=[pl.BlockSpec(memory_space=pltpu.SMEM)] + [vm] * (1 + len(got)),
        out_specs=[vm] * 3,
        out_shape=[
            jax.ShapeDtypeStruct((half, width), F32),
            jax.ShapeDtypeStruct((half + 16, width), BF),
            jax.ShapeDtypeStruct((16, width), F32),
        ],
        compiler_params=pltpu.CompilerParams(vmem_limit_bytes=48 << 20),
        cost_estimate=LIGHT,
    )(side.reshape(1, 1), first, *got)


def add_near_kernel(a, c, got, out_in, out_out):
    out_in[0] = a[0] + jnp.transpose(got[0, 0].astype(F32))
    out_out[0] = c[0] + got[0, 1].astype(F32)


def add_near(dwi_own, dwo_own, got):
    le, width, hidden = dwi_own.shape
    tile = 256
    turned = pl.BlockSpec((1, width, tile), lambda j, c: (j, 0, c))
    plain = pl.BlockSpec((1, tile, width), lambda j, c: (j, c, 0))
    both = pl.BlockSpec((1, 2, tile, width), lambda j, c: (j, 0, c, 0))
    return pl.pallas_call(
        add_near_kernel,
        grid=(le, hidden // tile),
        in_specs=[turned, plain, both],
        out_specs=[turned, plain],
        out_shape=[jax.ShapeDtypeStruct(dwi_own.shape, F32), jax.ShapeDtypeStruct(dwo_own.shape, F32)],
        input_output_aliases={0: 0, 1: 1},
        cost_estimate=LIGHT,
    )(dwi_own, dwo_own, got)


def side_of(array, place):
    return place[0] if array.shape[0] > 1 else 0


def mixed_norm_kernel(rows, back, gain, shift, out):
    normal, _ = normal_of(rows[0, 0].astype(F32) + back[0].astype(F32))
    out[0] = (normal * gain[...] + shift[...]).astype(BF)


def mixed_norm(t, rows, back, gain, shift):
    le, n, width = back.shape
    block = pl.BlockSpec((1, 128, width), lambda j, c: (j, c, 0))
    line = pl.BlockSpec((1, width), lambda j, c: (0, 0))
    return pl.pallas_call(
        mixed_norm_kernel,
        grid=(le, n // 128),
        in_specs=[pl.BlockSpec((1, 1, 128, width), lambda j, c: (t, j, c, 0)), block, line, line],
        out_specs=block,
        out_shape=jax.ShapeDtypeStruct((le, n, width), BF),
        cost_estimate=LIGHT,
    )(rows, back, gain, shift)


def mixed_back_kernel(_, rows, back, gx, gx_far, cot, fill, gain, exact, low, sums):
    @pl.when((pl.program_id(0) == 0) & (pl.program_id(1) == 0))
    def _():
        sums[...] = jnp.zeros_like(sums)

    normal, inverse = normal_of(rows[0, 0].astype(F32) + back[0].astype(F32))
    g = gx[0].astype(F32) + gx_far[0, 0].astype(F32)
    sums[0:1, :] += jnp.sum(g * normal, axis=0, keepdims=True)
    sums[1:2, :] += jnp.sum(g, axis=0, keepdims=True)
    u = g * gain[...]
    total = cot[0, 0].astype(F32) * fill[0] + inverse * (
        u - jnp.mean(u, axis=-1, keepdims=True) - normal * jnp.mean(u * normal, axis=-1, keepdims=True)
    )
    exact[0] = total
    low[0] = total.astype(BF)


def mixed_back(t, other, rows, back, gx, gx_far, cot, fill, gain):
    le, n, width = back.shape
    block = pl.BlockSpec((1, 128, width), lambda j, c, s: (j, c, 0))
    whole = pl.BlockSpec((1, 1, 128, width), lambda j, c, s: (t, j, c, 0))
    return pl.pallas_call(
        mixed_back_kernel,
        grid_spec=pltpu.PrefetchScalarGridSpec(
            num_scalar_prefetch=1,
            grid=(le, n // 128),
            in_specs=[
                whole, block, block,
                pl.BlockSpec((1, 1, 128, width), lambda j, c, s: (side_of(gx_far, s), j, c, 0)),
                whole,
                pl.BlockSpec((1, 128, 1), lambda j, c, s: (j, c, 0)),
                pl.BlockSpec((1, width), lambda j, c, s: (0, 0)),
            ],
            out_specs=[block, block, pl.BlockSpec((8, width), lambda j, c, s: (0, 0))],
        ),
        out_shape=[
            jax.ShapeDtypeStruct((le, n, width), F32),
            jax.ShapeDtypeStruct((le, n, width), BF),
            jax.ShapeDtypeStruct((8, width), F32),
        ],
        cost_estimate=LIGHT,
    )(other, rows, back, gx, gx_far, cot, fill, gain)


def gelu_parts(v):
    a, b = 0.7978845608028654, 0.044715
    square = v * v
    t = jnp.tanh(a * v * (1.0 + b * square))
    half = 0.5 * (1.0 + t)
    slope = half + 0.5 * v * (1.0 - t * t) * (a * (1.0 + 3.0 * b * square))
    return v * half, slope


def expert_kernel(first, tiles, _, *refs):
    (x_own, x_far, g_own, g_far, fill_own, fill_far, wi_own, wi_near, wo_own, wo_near, bias) = refs[:11]
    before = [None] * 5 if first else refs[11:16]
    (out_own, out_far, gx_own, gx_far, dwi_own, dwo_own, dw_near, db, dbo,
     xs, gs, out_sum, gx_sum) = refs[11 if first else 16 :]
    h = pl.program_id(1)
    rows = x_own.shape[1]

    @pl.when(h == 0)
    def _():
        xs[:rows, :] = x_own[0]
        xs[rows:, :] = x_far[0, 0]
        total = None
        for start, ref, fill in ((0, g_own[0, 0], fill_own), (rows, g_far[0, 0, 0], fill_far)):
            g = ref.astype(F32) * fill[0]
            gs[start : start + rows, :] = g.astype(BF)
            part = jnp.sum(g, axis=0, keepdims=True)
            total = part if total is None else total + part
        out_sum[...] = jnp.zeros_like(out_sum)
        gx_sum[...] = jnp.zeros_like(gx_sum)
        dbo[0] = total if first else total + before[4][0]

    def tile_step(wi, wo, mine):
        x, g = xs[...], gs[...]
        inner = dot(x, wi, NN) + bias[0]
        act, slope = gelu_parts(inner)
        act = act.astype(BF)
        grad_inner = (dot(g, wo, NT) * slope).astype(BF)
        out_sum[...] += dot(act, wo, NN)
        gx_sum[...] += dot(grad_inner, wi, NT)
        dwi = dot(x, grad_inner, TN) if mine else dot(grad_inner, x, TN)
        dwo = dot(act, g, TN)
        column = jnp.sum(grad_inner.astype(F32), axis=0, keepdims=True)
        if mine:
            dwi_own[0] = dwi.astype(BF) if first else dwi + before[0][0].astype(F32)
            dwo_own[0] = dwo.astype(BF) if first else dwo + before[1][0].astype(F32)
        else:
            dw_near[0, 0] = (dwi if first else dwi + before[2][0, 0].astype(F32)).astype(dw_near.dtype)
            dw_near[0, 1] = (dwo if first else dwo + before[2][0, 1].astype(F32)).astype(dw_near.dtype)
        db[0] = column if first else column + before[3][0]

    @pl.when(h < tiles)
    def _():
        tile_step(wi_own[0], wo_own[0], True)

    @pl.when(h >= tiles)
    def _():
        tile_step(wi_near[0], wo_near[0], False)

    @pl.when(h == 2 * tiles - 1)
    def _():
        out_own[0] = out_sum[:rows, :].astype(BF)
        out_far[0] = out_sum[rows:, :].astype(BF)
        gx_own[0] = gx_sum[:rows, :].astype(BF)
        gx_far[0] = gx_sum[rows:, :].astype(BF)


def expert_step(t, other, x_own, x_far, g_own, g_far, fills, wi_own, wo_own, w_near, bias, before, tile=512):
    le, rows, width = x_own.shape
    hidden = wi_own.shape[2]
    tiles = hidden // tile
    first = before is None
    out_row = pl.BlockSpec((1, rows, width), lambda j, h, s: (j, 0, 0))
    mark = pl.BlockSpec((1, rows, 1), lambda j, h, s: (j, 0, 0))
    own = lambda h: jnp.minimum(h, tiles - 1)
    near = lambda h: jnp.maximum(h - tiles, 0)
    shapes = [jax.ShapeDtypeStruct((le, rows, width), BF)] * 4 + [
        jax.ShapeDtypeStruct((le, width, hidden), BF if first else F32),
        jax.ShapeDtypeStruct((le, hidden, width), BF if first else F32),
        jax.ShapeDtypeStruct((le, 2, hidden, width), BF),
        jax.ShapeDtypeStruct((le, 1, 2 * hidden), F32),
        jax.ShapeDtypeStruct((le, 1, width), F32),
    ]
    own_in = pl.BlockSpec((1, width, tile), lambda j, h, s: (j, 0, own(h)))
    own_out = pl.BlockSpec((1, tile, width), lambda j, h, s: (j, own(h), 0))
    column = pl.BlockSpec((1, 1, tile), lambda j, h, s: (j, 0, h))
    grads = [
        own_in,
        own_out,
        pl.BlockSpec((1, 2, tile, width), lambda j, h, s: (j, 0, near(h), 0)),
        column,
        pl.BlockSpec((1, 1, width), lambda j, h, s: (j, 0, 0)),
    ]
    operands = [x_own, x_far, g_own, g_far, *fills, wi_own, w_near, wo_own, w_near, bias]
    in_specs = [
        pl.BlockSpec((1, rows, width), lambda j, h, s: (j, 0, 0)),
        pl.BlockSpec((1, 1, rows, width), lambda j, h, s: (side_of(x_far, s), j, 0, 0)),
        pl.BlockSpec((1, 1, rows, width), lambda j, h, s: (t, j, 0, 0)),
        pl.BlockSpec((1, 1, 1, rows, width), lambda j, h, s: (side_of(g_far, s), t, j, 0, 0)),
        mark,
        mark,
        own_in,
        pl.BlockSpec((1, width, tile), lambda j, h, s: (j, 0, near(h))),
        own_out,
        pl.BlockSpec((1, tile, width), lambda j, h, s: (le + j, near(h), 0)),
        column,
    ]
    if not first:
        operands += list(before)
        in_specs += grads
    return pl.pallas_call(
        functools.partial(expert_kernel, first, tiles),
        grid_spec=pltpu.PrefetchScalarGridSpec(
            num_scalar_prefetch=1,
            grid=(le, 2 * tiles),
            in_specs=in_specs,
            out_specs=[out_row] * 4 + grads,
            scratch_shapes=[pltpu.VMEM((2 * rows, width), BF)] * 2 + [pltpu.VMEM((2 * rows, width), F32)] * 2,
        ),
        out_shape=shapes,
        compiler_params=pltpu.CompilerParams(vmem_limit_bytes=60 << 20),
        cost_estimate=LIGHT,
    )(other, *operands)


def pick(array, index, dim):
    return lax.dynamic_index_in_dim(array, index, dim, keepdims=False)


def after(array, *others):
    return lax.optimization_barrier((array,) + others)[0]


def crossed(n, step):
    return [(i, i ^ step) for i in range(n)]


def both_groups(array, n_f):
    pairs = [[i, i ^ 2] for i in range(n_f) if not i & 2]
    return lax.all_gather(array, "fsdp", axis_index_groups=pairs)


def gather_all(shard, first, n_exp, n_f, ex, fi, share):
    block, step = shard[None], 1
    while step < n_f:
        block = jnp.concatenate([block, lax.ppermute(block, "fsdp", crossed(n_f, step))])
        if step == 1:
            block = after(block, first)
        step *= 2
    pieces = [block] + [lax.ppermute(block, "exp", crossed(n_exp, 2 * k)) for k in range(1, n_exp // 2)]
    pieces += [lax.ppermute(piece, "exp", crossed(n_exp, 1)) for piece in pieces]
    return block, place_rows(pieces, ex, fi, share)


def body(
    block_input,
    expert_ids,
    seq_lengths,
    attn_norm_gain,
    attn_norm_bias,
    query_matrix,
    query_offset_bias,
    key_matrix,
    value_matrix,
    value_offset_bias,
    output_matrix,
    attention_output_bias,
    ffn_norm_gain,
    ffn_norm_bias,
    expert_in,
    expert_in_bias,
    expert_out,
    expert_out_bias,
    out_cotangent,
):
    mb, le, _, sources, cap, width = block_input.shape
    n_exp, n_f = lax.axis_size("exp"), lax.axis_size("fsdp")
    ex, fi = lax.axis_index("exp"), lax.axis_index("fsdp")
    chip, core = ex // 2, ex % 2
    everyone = ("exp", "fsdp")
    owners = n_exp * n_f
    experts = le * n_exp
    slots = experts * cap
    rows = sources * cap
    hidden = expert_in.shape[2]
    seq = expert_ids.shape[2]
    far, near = crossed(n_f, 2), crossed(n_f, 1)
    share = attn_norm_gain.shape[0]

    ids = expert_ids[:, 0, :, 0]
    onehot = ids[:, :, None] == jnp.arange(experts, dtype=jnp.int32)
    counts = jnp.sum(onehot.astype(F32), axis=1)
    position = jnp.arange(seq, dtype=jnp.int32)
    same = (ids[:, :, None] == ids[:, None, :]) & (position[None, None, :] < position[None, :, None])
    slot_ids = ids * cap + jnp.sum(same.astype(jnp.int32), axis=2)
    packed = jnp.concatenate(
        [
            attn_norm_gain,
            attn_norm_bias,
            query_offset_bias,
            value_offset_bias,
            attention_output_bias,
            ffn_norm_gain,
            ffn_norm_bias,
            expert_out_bias.reshape(-1),
            expert_in_bias.reshape(-1),
            counts.astype(BF).reshape(-1),
        ]
    )
    lines = -(-packed.size // (16 * width)) * 16
    packed = jnp.pad(packed, (0, lines * width - packed.size)).reshape(lines, width)
    shipped = jnp.concatenate([query_matrix, key_matrix, value_matrix, output_matrix, packed])
    arrived_all = [
        lax.all_to_all(block_input[t, :, 0], "exp", split_axis=1, concat_axis=0, tiled=True).reshape(slots, width)
        for t in range(mb)
    ]
    ready, (dense_full, table) = gather_all(shipped, arrived_all[0], n_exp, n_f, ex, fi, share)
    table = table.reshape(owners, -1).astype(F32)
    cot = out_cotangent[:, :, 0].reshape(mb, le, rows, width)
    other = (1 - (fi // 2) % 2).astype(jnp.int32).reshape(1)
    cot_far = both_groups(after(cot, ready), n_f)
    w_near = lax.ppermute(after(jnp.concatenate([expert_in, expert_out]), ready), "fsdp", near)
    block_rows = block_input[:, :, 0].reshape(mb, le, rows, width)

    small = jnp.stack(
        [table[:, i * share : (i + 1) * share].reshape(-1) for i in range(7)] + [jnp.zeros((width,), F32)]
    )
    at = 7 * share
    table = table.reshape(n_exp, n_f, -1)
    mine = pick(table, ex, 0)
    bias_out = mine[:, at : at + expert_out_bias.size].reshape(n_f, le, -1).transpose(1, 0, 2).reshape(le, width)
    at += expert_out_bias.size
    bias_in = mine[:, at : at + le * hidden].reshape(n_f, le, hidden)
    bias_in = jnp.concatenate([pick(bias_in, fi, 0), pick(bias_in, fi ^ 1, 0)], axis=1)[:, None, :]
    at += le * hidden
    my_counts = table[:, :, at : at + counts.size].reshape(n_exp, n_f, mb, n_exp, le)
    my_counts = pick(my_counts, ex, 3)

    def fill(group):
        count = pick(my_counts, group, 1).transpose(1, 2, 0)[:, :, :, None]
        return (jnp.arange(cap, dtype=F32) < count).astype(F32).reshape(mb, le, rows, 1)

    fill_own, fill_far = fill(fi), fill(fi ^ 2)

    saved, back_rows, normed_two = [], [], []
    for t in range(mb):
        placed, kept = attention_forward(arrived_all[t], slot_ids[t], seq_lengths[t, 0], dense_full, small)
        saved.append(kept)
        back_rows.append(
            lax.all_to_all(
                placed.reshape(experts, cap, width), "exp", split_axis=0, concat_axis=1, tiled=True
            ).reshape(le, rows, width)
        )
        normed_two.append(mixed_norm(t, block_rows, back_rows[t], small[5:6], small[6:7]))
    normed_far = [lax.ppermute(normed_two[0], "fsdp", far)[None]]
    for t in range(1, mb):
        rows_sent, cot_far = lax.optimization_barrier((normed_two[t], cot_far))
        normed_far.append(lax.ppermute(rows_sent, "fsdp", far)[None])

    ffn, before = [], None
    for t in range(mb):
        ffn.append(
            expert_step(
                t, other, normed_two[t], normed_far[t], cot, cot_far, (fill_own[t], fill_far[t]),
                expert_in, expert_out, w_near, bias_in, before,
            )
        )
        before = ffn[t][4:]
    gx_far = [lax.ppermute(ffn[0][3], "fsdp", far)[None]]
    for t in range(1, mb):
        gx_far.append(both_groups(after(ffn[t][3], gx_far[t - 1]), n_f))
    dwi_own, dwo_own, dw_near, db, dbo = before
    dbo = dbo[:, 0]
    vectors = jnp.concatenate([db[:, 0, hidden:], dbo], axis=1)

    dw_got = lax.ppermute(dw_near, "fsdp", near)
    input_grads, terms, small_total = [], [], None
    for t in range(mb):
        got = gx_far[t]
        if t == mb - 1:
            outs = jnp.stack([ffn[i][1] for i in range(mb)])
            got, outs, placed_back = lax.optimization_barrier((got, outs, placed_back))
            out_far = both_groups(outs, n_f)
        grad_mixed, to_send, norm_sums = mixed_back(
            t, other, block_rows, back_rows[t], ffn[t][2], got, cot, fill_own[t], small[5:6]
        )
        grad_arrived = lax.all_to_all(
            to_send.reshape(le, sources, cap, width), "exp", split_axis=1, concat_axis=0, tiled=True
        ).reshape(slots, width)
        placed_back, keep, give, sums = attention_backward(
            grad_arrived, slot_ids[t], seq_lengths[t, 0], core, dense_full, small, saved[t], owners, n_f
        )
        returned = lax.all_to_all(
            placed_back.reshape(experts, cap, width), "exp", split_axis=0, concat_axis=1, tiled=True
        ).reshape(le, rows, width)
        input_grads.append(
            (grad_mixed + returned.astype(F32)).astype(BF).reshape(le, 1, sources, cap, width)
        )
        sums = jnp.concatenate([sums[:5], norm_sums[:2], norm_sums[7:]])
        terms += list(keep) + [lax.ppermute(part, "exp", crossed(n_exp, 1)) for part in give]
        small_total = sums if t == 0 else small_total + sums

    sums_got = lax.ppermute(small_total, "exp", crossed(n_exp, 1))
    blocks = add_dense(terms, small_total, sums_got, chip, n_f)
    got = [lax.ppermute(blocks[k], "exp", crossed(n_exp, 2 * k)) for k in range(1, n_exp // 2)]
    keep, give, sums = add_plane((fi // 2) % 2, blocks[0], got)
    far_got = lax.ppermute(give, "fsdp", far)
    outputs = []
    far_outs = pick(out_far, other[0], 0)
    for t in range(mb):
        mixed = block_rows[t].astype(F32) + back_rows[t].astype(F32)
        ffn_out = ffn[t][0].astype(F32) + far_outs[t].astype(F32) + bias_out[:, None, :]
        outputs.append(
            ((mixed + ffn_out) * fill_own[t]).astype(BF).reshape(le, 1, sources, cap, width)
        )
    outputs = jnp.stack(outputs)
    half = keep.shape[0]
    keep = keep + far_got[:half].astype(F32)
    sums = sums + far_got[half:].astype(F32)
    pairs = keep.reshape(2, 4 * share, width)
    ride = jnp.pad(vectors, ((0, 0), (0, -vectors.shape[1] % width))).reshape(-1, width)
    give = jnp.concatenate([pick(pairs, 1 - fi % 2, 0), sums, ride]).astype(BF)
    give, outputs = lax.optimization_barrier((give, outputs))
    near_got = lax.ppermute(give, "fsdp", near).astype(F32)
    total = pick(pairs, fi % 2, 0) + near_got[: 4 * share]
    sums = sums + near_got[4 * share : 4 * share + 16]
    vectors_got = near_got[4 * share + 16 :].reshape(le, -1)[:, : vectors.shape[1]]
    grad_in, grad_out = add_near(dwi_own, dwo_own, dw_got)
    dense = total.reshape(4, share, width)
    smalls = lax.dynamic_slice_in_dim(sums, (ex * n_f + fi) * share, share, 1)

    grad_in_bias = db[:, 0, :hidden] + vectors_got[:, :hidden]
    grad_out_bias = lax.dynamic_slice_in_dim(
        dbo + vectors_got[:, hidden:], fi * (width // n_f), width // n_f, 1
    )
    return (
        outputs,
        jnp.stack(input_grads),
        smalls[0],
        smalls[1],
        dense[0],
        smalls[2],
        dense[1],
        dense[2],
        smalls[3],
        dense[3],
        smalls[4],
        smalls[5],
        smalls[6],
        grad_in,
        grad_in_bias,
        grad_out,
        grad_out_bias,
    )


def solution(mesh):
    rows, dense, vec = (
        P(None, "exp", "fsdp", None, None, None),
        P(("exp", "fsdp"), None),
        P(("exp", "fsdp")),
    )
    experts = (P("exp", None, "fsdp"), P("exp", "fsdp"), P("exp", "fsdp", None), P("exp", "fsdp"))
    return jax.shard_map(
        body,
        mesh=mesh,
        in_specs=(
            rows,
            P(None, ("exp", "fsdp"), None, None),
            P(None, ("exp", "fsdp")),
            vec,
            vec,
            dense,
            vec,
            dense,
            dense,
            vec,
            dense,
            vec,
            vec,
            vec,
        )
        + experts
        + (rows,),
        out_specs=(rows, rows, vec, vec, dense, vec, dense, dense, vec, dense, vec, vec, vec) + experts,
        check_vma=False,
    )
```

```python
import functools
import math

import jax
import jax.numpy as jnp
from jax import lax
from jax.experimental import pallas as pl
from jax.experimental.pallas import tpu as pltpu
from jax.sharding import PartitionSpec as P

HEADS = 16
BF = jnp.bfloat16
F32 = jnp.float32


def dot(a, b, dims):
    return lax.dot_general(a, b, (dims, ((), ())), preferred_element_type=F32)


LIGHT = pl.CostEstimate(flops=1_000_000, bytes_accessed=100_000, transcendentals=0)
NN, NT, TN = ((1,), (0,)), ((1,), (1,)), ((0,), (0,))


def iota(shape, dim):
    return lax.broadcasted_iota(jnp.int32, shape, dim)


def chosen(condition):
    return jnp.where(condition, 1.0, 0.0).astype(BF)


def half_lanes(block, sub):
    lane = iota(block.shape, 1)
    width = block.shape[1] // 2
    inside = (lane < width) if sub == 0 else (lane >= width)
    return jnp.where(inside, block.astype(F32), 0.0).astype(BF)


def normal_of(rows):
    average = jnp.mean(rows, axis=-1, keepdims=True)
    centred = rows - average
    inverse = lax.rsqrt(jnp.mean(centred * centred, axis=-1, keepdims=True) + 1e-05)
    return centred * inverse, inverse


def fill_bias(bias, length):
    seq = bias.shape[0]
    query, key = iota((seq, seq), 0), iota((seq, seq), 1)
    bias[...] = jnp.where((key <= query) & (key < length), 0.0, -1e30)


def query_blocks(seq):
    block = 256 if seq % 256 == 0 else seq
    return [(start, block, start + block) for start in range(0, seq, block)]


def forward_kernel(
    length, column, row, arrived, w, small, placed, rows_out, q_out, k_out, v_out, att_out, lse_out, bias, normed
):
    slots, width = arrived.shape
    seq = column.shape[0]
    head = width // HEADS
    scale = head**-0.5
    fill_bias(bias, length[0, 0])
    chunk, tile = 128, 256

    @pl.loop(0, seq // chunk)
    def _(c):
        at = pl.ds(pl.multiple_of(c * chunk, chunk), chunk)
        pick = chosen(column[at, :] == iota((chunk, slots), 1))
        rows = dot(pick, arrived[...], NN)
        rows_out[at, :] = rows.astype(BF)
        normal, _ = normal_of(rows)
        normed[at, :] = (normal * small[0:1, :] + small[1:2, :]).astype(BF)

    @pl.loop(0, width // tile)
    def _(n):
        at = pl.ds(pl.multiple_of(n * tile, tile), tile)
        x = normed[...]
        q_out[:, at] = (dot(x, w[0, :, at], NN) + small[2:3, at]).astype(BF)
        k_out[:, at] = dot(x, w[1, :, at], NN).astype(BF)
        v_out[:, at] = (dot(x, w[2, :, at], NN) + small[3:4, at]).astype(BF)

    @pl.loop(0, HEADS // 2)
    def _(pair):
        at = pl.ds(pl.multiple_of(pair * 2 * head, 2 * head), 2 * head)
        k2, v2 = k_out[:, at], v_out[:, at]
        values = [half_lanes(v2, sub) for sub in (0, 1)]
        for start, size, reach in query_blocks(seq):
            q2 = q_out[start : start + size, at]
            total = None
            lse_block = lse_out[start : start + size, :]
            lane = iota(lse_block.shape, 1)
            for sub in (0, 1):
                s = dot(half_lanes(q2, sub), k2[:reach], NT) * scale + bias[start : start + size, :reach]
                top = jnp.max(s, axis=-1, keepdims=True)
                p = jnp.exp(s - top)
                l = jnp.sum(p, axis=-1, keepdims=True)
                out = dot((p * (1.0 / l)).astype(BF), values[sub][:reach], NN)
                total = out if sub == 0 else total + out
                lse_block = jnp.where(lane == 2 * pair + sub, top + jnp.log(l), lse_block)
            att_out[start : start + size, at] = total.astype(BF)
            lse_out[start : start + size, :] = lse_block

    @pl.loop(0, width // tile)
    def _(n):
        at = pl.ds(pl.multiple_of(n * tile, tile), tile)
        normed[:, at] = (dot(att_out[...], w[3, :, at], NN) + small[4:5, at]).astype(BF)

    @pl.loop(0, slots // chunk)
    def _(c):
        at = pl.ds(pl.multiple_of(c * chunk, chunk), chunk)
        put = chosen(row[...] == iota((chunk, seq), 0) + c * chunk)
        placed[at, :] = dot(put, normed[...], NN).astype(BF)


def attention_forward(arrived, slot_ids, length, w, small):
    slots, width = arrived.shape
    seq = slot_ids.shape[0]
    wide = jax.ShapeDtypeStruct((seq, width), BF)
    vm = pl.BlockSpec(memory_space=pltpu.VMEM)
    out = pl.pallas_call(
        forward_kernel,
        in_specs=[pl.BlockSpec(memory_space=pltpu.SMEM)] + [vm] * 5,
        out_specs=[vm] * 7,
        out_shape=[jax.ShapeDtypeStruct((slots, width), BF)]
        + [wide] * 5
        + [jax.ShapeDtypeStruct((seq, 128), F32)],
        scratch_shapes=[pltpu.VMEM((seq, seq), F32), pltpu.VMEM((seq, width), BF)],
        compiler_params=pltpu.CompilerParams(vmem_limit_bytes=48 << 20),
        cost_estimate=LIGHT,
    )(length.reshape(1, 1), slot_ids.reshape(seq, 1), slot_ids.reshape(1, seq), arrived, w, small)
    return out[0], tuple(out[1:])


def backward_kernel(
    groups, length, core, column, row, arrived, w, small, rows_in, q, k, v, att, lse,
    placed, *rest,
):
    keep, give, sums = rest[:4], rest[4:8], rest[8]
    bias, normed, grad_out, grad_att, dq, dk, dv, grad_normed = rest[9:]
    slots, width = arrived.shape
    seq = column.shape[0]
    head = width // HEADS
    scale = head**-0.5
    fill_bias(bias, length[0, 0])
    chunk, tile = 128, 256
    sums[...] = jnp.zeros_like(sums)

    @pl.loop(0, seq // chunk)
    def _(c):
        at = pl.ds(pl.multiple_of(c * chunk, chunk), chunk)
        pick = chosen(column[at, :] == iota((chunk, slots), 1))
        rows = dot(pick, arrived[...], NN)
        grad_out[at, :] = rows.astype(BF)
        sums[4:5, :] += jnp.sum(rows, axis=0, keepdims=True)
        normal, _ = normal_of(rows_in[at, :].astype(F32))
        normed[at, :] = (normal * small[0:1, :] + small[1:2, :]).astype(BF)

    @pl.loop(0, width // tile)
    def _(n):
        at = pl.ds(pl.multiple_of(n * tile, tile), tile)
        grad_att[:, at] = dot(grad_out[...], w[3, at, :], NT).astype(BF)

    @pl.loop(0, HEADS // 2)
    def _(pair):
        at = pl.ds(pl.multiple_of(pair * 2 * head, 2 * head), 2 * head)
        k2, v2 = k[:, at], v[:, at]
        keys = [half_lanes(k2, sub) for sub in (0, 1)]
        dks, dvs = [], []
        for start, size, reach in query_blocks(seq):
            span = slice(start, start + size)
            q2, g2, lse_block = q[span, at], grad_att[span, at], lse[span, :]
            lane = iota(lse_block.shape, 1)
            dq_total = dk_total = dv_total = None
            for sub in (0, 1):
                qs, gs = half_lanes(q2, sub), half_lanes(g2, sub)
                level = jnp.sum(jnp.where(lane == 2 * pair + sub, lse_block, 0.0), axis=-1, keepdims=True)
                s = dot(qs, k2[:reach], NT) * scale + bias[span, :reach]
                p = jnp.exp(s - level)
                dp = dot(gs, v2[:reach], NT)
                mean = jnp.sum(p * dp, axis=-1, keepdims=True)
                ds = (p * (dp - mean)).astype(BF)
                parts = (dot(ds, keys[sub][:reach], NN), dot(ds, qs, TN), dot(p.astype(BF), gs, TN))
                if sub == 0:
                    dq_total, dk_total, dv_total = parts
                else:
                    dq_total, dk_total, dv_total = (
                        dq_total + parts[0], dk_total + parts[1], dv_total + parts[2]
                    )
            dq[span, at] = (dq_total * scale).astype(BF)
            dks.append((reach, dk_total))
            dvs.append((reach, dv_total))
        for ref, pieces, factor in ((dk, dks, scale), (dv, dvs, 1.0)):
            before = 0
            for index, (reach, _) in enumerate(pieces):
                total = sum(piece[before:reach] for _, piece in pieces[index:])
                ref[before:reach, at] = (total * factor).astype(BF)
                before = reach

    for m, (left, right) in enumerate(((normed, dq), (normed, dk), (normed, dv), (att, grad_out))):
        write_dense(groups, keep[m], give[m], core, left, right)

    @pl.loop(0, width // tile)
    def _(n):
        at = pl.ds(pl.multiple_of(n * tile, tile), tile)
        grad_normed[:, at] = (
            dot(dq[...], w[0, at, :], NT) + dot(dk[...], w[1, at, :], NT) + dot(dv[...], w[2, at, :], NT)
        )

    @pl.loop(0, seq // chunk)
    def _(c):
        at = pl.ds(pl.multiple_of(c * chunk, chunk), chunk)
        normal, inverse = normal_of(rows_in[at, :].astype(F32))
        g = grad_normed[at, :]
        sums[0:1, :] += jnp.sum(g * normal, axis=0, keepdims=True)
        sums[1:2, :] += jnp.sum(g, axis=0, keepdims=True)
        sums[2:3, :] += jnp.sum(dq[at, :].astype(F32), axis=0, keepdims=True)
        sums[3:4, :] += jnp.sum(dv[at, :].astype(F32), axis=0, keepdims=True)
        u = g * small[0:1, :]
        back = inverse * (
            u - jnp.mean(u, axis=-1, keepdims=True) - normal * jnp.mean(u * normal, axis=-1, keepdims=True)
        )
        grad_out[at, :] = back.astype(BF)

    @pl.loop(0, slots // chunk)
    def _(c):
        at = pl.ds(pl.multiple_of(c * chunk, chunk), chunk)
        put = chosen(row[...] == iota((chunk, seq), 0) + c * chunk)
        placed[at, :] = dot(put, grad_out[...], NN).astype(BF)


def write_dense(groups, keep, give, core, left, right):
    width = right.shape[1]
    share = width // (2 * keep.shape[0])
    side = share * groups
    pieces = max(2 * side, 128) // side

    @pl.loop(0, width // (side * pieces))
    def _(step):
        at = pl.ds(pl.multiple_of(step * side * pieces, side * pieces), side * pieces)
        block = dot(left[:, at], right[...], TN).astype(BF).reshape(pieces, groups, share, width)
        for i in range(pieces):
            to = pl.ds((step * (pieces // 2) + i // 2) * groups, groups)

            @pl.when(core[0, 0] == i % 2)
            def _():
                keep[to] = block[i]

            @pl.when(core[0, 0] != i % 2)
            def _():
                give[to] = block[i]


def attention_backward(arrived, slot_ids, length, core, w, small, saved, owners, groups):
    slots, width = arrived.shape
    seq = slot_ids.shape[0]
    vm = pl.BlockSpec(memory_space=pltpu.VMEM)
    sm = pl.BlockSpec(memory_space=pltpu.SMEM)
    half = jax.ShapeDtypeStruct((owners // 2, width // owners, width), BF)
    out = pl.pallas_call(
        functools.partial(backward_kernel, groups),
        in_specs=[sm, sm] + [vm] * 11,
        out_specs=[vm] * 10,
        out_shape=[jax.ShapeDtypeStruct((slots, width), BF)] + [half] * 8 + [jax.ShapeDtypeStruct((8, width), F32)],
        scratch_shapes=[pltpu.VMEM((seq, seq), F32)]
        + [pltpu.VMEM((seq, width), BF)] * 6
        + [pltpu.VMEM((seq, width), F32)],
        compiler_params=pltpu.CompilerParams(vmem_limit_bytes=60 << 20),
        cost_estimate=LIGHT,
    )(
        length.reshape(1, 1), core.reshape(1, 1), slot_ids.reshape(seq, 1), slot_ids.reshape(1, seq),
        arrived, w, small, *saved,
    )
    return out[0], out[1:5], out[5:9], out[9]


def place_kernel(n_f, share, place, *refs):
    pieces, dense, table = refs[:-2], refs[-2], refs[-1]
    chips = len(pieces) // 2
    ex, fi = place[0, 0], place[0, 1]
    for c in range(2):
        for k in range(chips):
            for r in range(n_f):
                owner = jnp.bitwise_xor(ex, 2 * k + c) * n_f + jnp.bitwise_xor(fi, r)
                piece = pieces[c * chips + k]
                rows = pl.ds(pl.multiple_of(owner * share, share), share)
                for m in range(4):
                    dense[m, rows, :] = piece[r, m * share : (m + 1) * share, :]
                table[owner] = piece[r, 4 * share :, :]


def place_rows(pieces, ex, fi, share):
    n_f, lines, width = pieces[0].shape
    owners = len(pieces) * n_f
    vm = pl.BlockSpec(memory_space=pltpu.VMEM)
    return pl.pallas_call(
        functools.partial(place_kernel, n_f, share),
        in_specs=[pl.BlockSpec(memory_space=pltpu.SMEM)] + [vm] * len(pieces),
        out_specs=[vm] * 2,
        out_shape=[
            jax.ShapeDtypeStruct((4, owners * share, width), BF),
            jax.ShapeDtypeStruct((owners, lines - 4 * share, width), BF),
        ],
        compiler_params=pltpu.CompilerParams(vmem_limit_bytes=40 << 20),
        cost_estimate=LIGHT,
    )(jnp.stack([ex, fi]).astype(jnp.int32).reshape(1, 2), *pieces)


def rows_of(blocks):
    return blocks.reshape(-1, blocks.shape[-1])


def add_dense_kernel(groups, place, *refs):
    chips = refs[0].shape[0] // groups
    outs, (sums, got), terms = refs[-chips:], refs[-chips - 2 : -chips], refs[: -chips - 2]
    share = terms[0].shape[1]
    small = sums[...] + got[...]
    for k, out in enumerate(outs):
        owner = jnp.bitwise_xor(place[0, 0], k) * groups
        for f in range(groups):
            for m in range(4):
                total = sum(ref[owner + f].astype(F32) for ref in terms[m::4])
                at = (f * 4 + m) * share
                out[at : at + share, :] = total.astype(BF)
        out[groups * 4 * share :, :] = jnp.concatenate([small, jnp.zeros_like(small)]).astype(BF)


def add_dense(terms, sums, sums_got, chip, groups):
    count, share, width = terms[0].shape
    vm = pl.BlockSpec(memory_space=pltpu.VMEM)
    out = jax.ShapeDtypeStruct((groups * 4 * share + 16, width), BF)
    return pl.pallas_call(
        functools.partial(add_dense_kernel, groups),
        in_specs=[pl.BlockSpec(memory_space=pltpu.SMEM)] + [vm] * (len(terms) + 2),
        out_specs=[vm] * (count // groups),
        out_shape=[out] * (count // groups),
        compiler_params=pltpu.CompilerParams(vmem_limit_bytes=48 << 20),
        cost_estimate=LIGHT,
    )(chip.reshape(1, 1), *terms, sums, sums_got)


def add_plane_kernel(side, first, *refs):
    got, (keep, give, sums) = refs[:-3], refs[-3:]
    half = keep.shape[0]

    def total(at, n):
        at = at if isinstance(at, int) else pl.multiple_of(at, 16)
        return sum((ref[pl.ds(at, n), :].astype(F32) for ref in got), first[pl.ds(at, n), :].astype(F32))

    step = 128 if half % 128 == 0 else half
    for at in range(0, half, step):
        keep[at : at + step, :] = total(side[0, 0] * half + at, step)
        give[at : at + step, :] = total((1 - side[0, 0]) * half + at, step).astype(BF)
    small = total(2 * half, 16)
    sums[...] = small
    give[half:, :] = small.astype(BF)


def add_plane(side, first, got):
    lines, width = first.shape
    half = (lines - 16) // 2
    vm = pl.BlockSpec(memory_space=pltpu.VMEM)
    return pl.pallas_call(
        add_plane_kernel,
        in_specs=[pl.BlockSpec(memory_space=pltpu.SMEM)] + [vm] * (1 + len(got)),
        out_specs=[vm] * 3,
        out_shape=[
            jax.ShapeDtypeStruct((half, width), F32),
            jax.ShapeDtypeStruct((half + 16, width), BF),
            jax.ShapeDtypeStruct((16, width), F32),
        ],
        compiler_params=pltpu.CompilerParams(vmem_limit_bytes=48 << 20),
        cost_estimate=LIGHT,
    )(side.reshape(1, 1), first, *got)


def add_near_kernel(a, c, got, out_in, out_out):
    out_in[0] = a[0] + jnp.transpose(got[0, 0].astype(F32))
    out_out[0] = c[0] + got[0, 1].astype(F32)


def add_near(dwi_own, dwo_own, got):
    le, width, hidden = dwi_own.shape
    tile = 256
    turned = pl.BlockSpec((1, width, tile), lambda j, c: (j, 0, c))
    plain = pl.BlockSpec((1, tile, width), lambda j, c: (j, c, 0))
    both = pl.BlockSpec((1, 2, tile, width), lambda j, c: (j, 0, c, 0))
    return pl.pallas_call(
        add_near_kernel,
        grid=(le, hidden // tile),
        in_specs=[turned, plain, both],
        out_specs=[turned, plain],
        out_shape=[jax.ShapeDtypeStruct(dwi_own.shape, F32), jax.ShapeDtypeStruct(dwo_own.shape, F32)],
        input_output_aliases={0: 0, 1: 1},
        cost_estimate=LIGHT,
    )(dwi_own, dwo_own, got)


def side_of(array, place):
    return place[0] if array.shape[0] > 1 else 0


def mixed_norm_kernel(rows, back, gain, shift, out):
    normal, _ = normal_of(rows[0, 0].astype(F32) + back[0].astype(F32))
    out[0] = (normal * gain[...] + shift[...]).astype(BF)


def mixed_norm(t, rows, back, gain, shift):
    le, n, width = back.shape
    block = pl.BlockSpec((1, 128, width), lambda j, c: (j, c, 0))
    line = pl.BlockSpec((1, width), lambda j, c: (0, 0))
    return pl.pallas_call(
        mixed_norm_kernel,
        grid=(le, n // 128),
        in_specs=[pl.BlockSpec((1, 1, 128, width), lambda j, c: (t, j, c, 0)), block, line, line],
        out_specs=block,
        out_shape=jax.ShapeDtypeStruct((le, n, width), BF),
        cost_estimate=LIGHT,
    )(rows, back, gain, shift)


def mixed_back_kernel(_, rows, back, gx, gx_far, cot, fill, gain, exact, low, sums):
    @pl.when((pl.program_id(0) == 0) & (pl.program_id(1) == 0))
    def _():
        sums[...] = jnp.zeros_like(sums)

    normal, inverse = normal_of(rows[0, 0].astype(F32) + back[0].astype(F32))
    g = gx[0].astype(F32) + gx_far[0, 0].astype(F32)
    sums[0:1, :] += jnp.sum(g * normal, axis=0, keepdims=True)
    sums[1:2, :] += jnp.sum(g, axis=0, keepdims=True)
    u = g * gain[...]
    total = cot[0, 0].astype(F32) * fill[0] + inverse * (
        u - jnp.mean(u, axis=-1, keepdims=True) - normal * jnp.mean(u * normal, axis=-1, keepdims=True)
    )
    exact[0] = total
    low[0] = total.astype(BF)


def mixed_back(t, other, rows, back, gx, gx_far, cot, fill, gain):
    le, n, width = back.shape
    block = pl.BlockSpec((1, 128, width), lambda j, c, s: (j, c, 0))
    whole = pl.BlockSpec((1, 1, 128, width), lambda j, c, s: (t, j, c, 0))
    return pl.pallas_call(
        mixed_back_kernel,
        grid_spec=pltpu.PrefetchScalarGridSpec(
            num_scalar_prefetch=1,
            grid=(le, n // 128),
            in_specs=[
                whole, block, block,
                pl.BlockSpec((1, 1, 128, width), lambda j, c, s: (side_of(gx_far, s), j, c, 0)),
                whole,
                pl.BlockSpec((1, 128, 1), lambda j, c, s: (j, c, 0)),
                pl.BlockSpec((1, width), lambda j, c, s: (0, 0)),
            ],
            out_specs=[block, block, pl.BlockSpec((8, width), lambda j, c, s: (0, 0))],
        ),
        out_shape=[
            jax.ShapeDtypeStruct((le, n, width), F32),
            jax.ShapeDtypeStruct((le, n, width), BF),
            jax.ShapeDtypeStruct((8, width), F32),
        ],
        cost_estimate=LIGHT,
    )(other, rows, back, gx, gx_far, cot, fill, gain)


def gelu_parts(v):
    a, b = 0.7978845608028654, 0.044715
    square = v * v
    t = jnp.tanh(a * v * (1.0 + b * square))
    half = 0.5 * (1.0 + t)
    slope = half + 0.5 * v * (1.0 - t * t) * (a * (1.0 + 3.0 * b * square))
    return v * half, slope


def expert_kernel(first, tiles, _, *refs):
    (x_own, x_far, g_own, g_far, fill_own, fill_far, wi_own, wi_near, wo_own, wo_near, bias) = refs[:11]
    before = [None] * 5 if first else refs[11:16]
    (out_own, out_far, gx_own, gx_far, dwi_own, dwo_own, dw_near, db, dbo,
     xs, gs, out_sum, gx_sum) = refs[11 if first else 16 :]
    h = pl.program_id(1)
    rows = x_own.shape[1]

    @pl.when(h == 0)
    def _():
        xs[:rows, :] = x_own[0]
        xs[rows:, :] = x_far[0, 0]
        total = None
        for start, ref, fill in ((0, g_own[0, 0], fill_own), (rows, g_far[0, 0, 0], fill_far)):
            g = ref.astype(F32) * fill[0]
            gs[start : start + rows, :] = g.astype(BF)
            part = jnp.sum(g, axis=0, keepdims=True)
            total = part if total is None else total + part
        out_sum[...] = jnp.zeros_like(out_sum)
        gx_sum[...] = jnp.zeros_like(gx_sum)
        dbo[0] = total if first else total + before[4][0]

    def tile_step(wi, wo, mine):
        x, g = xs[...], gs[...]
        inner = dot(x, wi, NN) + bias[0]
        act, slope = gelu_parts(inner)
        act = act.astype(BF)
        grad_inner = (dot(g, wo, NT) * slope).astype(BF)
        out_sum[...] += dot(act, wo, NN)
        gx_sum[...] += dot(grad_inner, wi, NT)
        dwi = dot(x, grad_inner, TN) if mine else dot(grad_inner, x, TN)
        dwo = dot(act, g, TN)
        column = jnp.sum(grad_inner.astype(F32), axis=0, keepdims=True)
        if mine:
            dwi_own[0] = dwi.astype(BF) if first else dwi + before[0][0].astype(F32)
            dwo_own[0] = dwo.astype(BF) if first else dwo + before[1][0].astype(F32)
        else:
            dw_near[0, 0] = (dwi if first else dwi + before[2][0, 0].astype(F32)).astype(dw_near.dtype)
            dw_near[0, 1] = (dwo if first else dwo + before[2][0, 1].astype(F32)).astype(dw_near.dtype)
        db[0] = column if first else column + before[3][0]

    @pl.when(h < tiles)
    def _():
        tile_step(wi_own[0], wo_own[0], True)

    @pl.when(h >= tiles)
    def _():
        tile_step(wi_near[0], wo_near[0], False)

    @pl.when(h == 2 * tiles - 1)
    def _():
        out_own[0] = out_sum[:rows, :].astype(BF)
        out_far[0] = out_sum[rows:, :].astype(BF)
        gx_own[0] = gx_sum[:rows, :].astype(BF)
        gx_far[0] = gx_sum[rows:, :].astype(BF)


def expert_step(t, other, x_own, x_far, g_own, g_far, fills, wi_own, wo_own, w_near, bias, before, tile=512):
    le, rows, width = x_own.shape
    hidden = wi_own.shape[2]
    tiles = hidden // tile
    first = before is None
    out_row = pl.BlockSpec((1, rows, width), lambda j, h, s: (j, 0, 0))
    mark = pl.BlockSpec((1, rows, 1), lambda j, h, s: (j, 0, 0))
    own = lambda h: jnp.minimum(h, tiles - 1)
    near = lambda h: jnp.maximum(h - tiles, 0)
    shapes = [jax.ShapeDtypeStruct((le, rows, width), BF)] * 4 + [
        jax.ShapeDtypeStruct((le, width, hidden), BF if first else F32),
        jax.ShapeDtypeStruct((le, hidden, width), BF if first else F32),
        jax.ShapeDtypeStruct((le, 2, hidden, width), BF),
        jax.ShapeDtypeStruct((le, 1, 2 * hidden), F32),
        jax.ShapeDtypeStruct((le, 1, width), F32),
    ]
    own_in = pl.BlockSpec((1, width, tile), lambda j, h, s: (j, 0, own(h)))
    own_out = pl.BlockSpec((1, tile, width), lambda j, h, s: (j, own(h), 0))
    column = pl.BlockSpec((1, 1, tile), lambda j, h, s: (j, 0, h))
    grads = [
        own_in,
        own_out,
        pl.BlockSpec((1, 2, tile, width), lambda j, h, s: (j, 0, near(h), 0)),
        column,
        pl.BlockSpec((1, 1, width), lambda j, h, s: (j, 0, 0)),
    ]
    operands = [x_own, x_far, g_own, g_far, *fills, wi_own, w_near, wo_own, w_near, bias]
    in_specs = [
        pl.BlockSpec((1, rows, width), lambda j, h, s: (j, 0, 0)),
        pl.BlockSpec((1, 1, rows, width), lambda j, h, s: (side_of(x_far, s), j, 0, 0)),
        pl.BlockSpec((1, 1, rows, width), lambda j, h, s: (t, j, 0, 0)),
        pl.BlockSpec((1, 1, 1, rows, width), lambda j, h, s: (side_of(g_far, s), t, j, 0, 0)),
        mark,
        mark,
        own_in,
        pl.BlockSpec((1, width, tile), lambda j, h, s: (j, 0, near(h))),
        own_out,
        pl.BlockSpec((1, tile, width), lambda j, h, s: (le + j, near(h), 0)),
        column,
    ]
    if not first:
        operands += list(before)
        in_specs += grads
    return pl.pallas_call(
        functools.partial(expert_kernel, first, tiles),
        grid_spec=pltpu.PrefetchScalarGridSpec(
            num_scalar_prefetch=1,
            grid=(le, 2 * tiles),
            in_specs=in_specs,
            out_specs=[out_row] * 4 + grads,
            scratch_shapes=[pltpu.VMEM((2 * rows, width), BF)] * 2 + [pltpu.VMEM((2 * rows, width), F32)] * 2,
        ),
        out_shape=shapes,
        compiler_params=pltpu.CompilerParams(vmem_limit_bytes=60 << 20),
        cost_estimate=LIGHT,
    )(other, *operands)


def pick(array, index, dim):
    return lax.dynamic_index_in_dim(array, index, dim, keepdims=False)


def after(array, *others):
    return lax.optimization_barrier((array,) + others)[0]


def crossed(n, step):
    return [(i, i ^ step) for i in range(n)]


def both_groups(array, n_f):
    pairs = [[i, i ^ 2] for i in range(n_f) if not i & 2]
    return lax.all_gather(array, "fsdp", axis_index_groups=pairs)


def gather_all(shard, first, n_exp, n_f, ex, fi, share):
    block, step = shard[None], 1
    while step < n_f:
        block = jnp.concatenate([block, lax.ppermute(block, "fsdp", crossed(n_f, step))])
        if step == 1:
            block = after(block, first)
        step *= 2
    pieces = [block] + [lax.ppermute(block, "exp", crossed(n_exp, 2 * k)) for k in range(1, n_exp // 2)]
    pieces += [lax.ppermute(piece, "exp", crossed(n_exp, 1)) for piece in pieces]
    return block, place_rows(pieces, ex, fi, share)


def body(
    block_input,
    expert_ids,
    seq_lengths,
    attn_norm_gain,
    attn_norm_bias,
    query_matrix,
    query_offset_bias,
    key_matrix,
    value_matrix,
    value_offset_bias,
    output_matrix,
    attention_output_bias,
    ffn_norm_gain,
    ffn_norm_bias,
    expert_in,
    expert_in_bias,
    expert_out,
    expert_out_bias,
    out_cotangent,
):
    mb, le, _, sources, cap, width = block_input.shape
    n_exp, n_f = lax.axis_size("exp"), lax.axis_size("fsdp")
    ex, fi = lax.axis_index("exp"), lax.axis_index("fsdp")
    chip, core = ex // 2, ex % 2
    everyone = ("exp", "fsdp")
    owners = n_exp * n_f
    experts = le * n_exp
    slots = experts * cap
    rows = sources * cap
    hidden = expert_in.shape[2]
    seq = expert_ids.shape[2]
    far, near = crossed(n_f, 2), crossed(n_f, 1)
    share = attn_norm_gain.shape[0]

    ids = expert_ids[:, 0, :, 0]
    onehot = ids[:, :, None] == jnp.arange(experts, dtype=jnp.int32)
    counts = jnp.sum(onehot.astype(F32), axis=1)
    position = jnp.arange(seq, dtype=jnp.int32)
    same = (ids[:, :, None] == ids[:, None, :]) & (position[None, None, :] < position[None, :, None])
    slot_ids = ids * cap + jnp.sum(same.astype(jnp.int32), axis=2)
    packed = jnp.concatenate(
        [
            attn_norm_gain,
            attn_norm_bias,
            query_offset_bias,
            value_offset_bias,
            attention_output_bias,
            ffn_norm_gain,
            ffn_norm_bias,
            expert_out_bias.reshape(-1),
            expert_in_bias.reshape(-1),
            counts.astype(BF).reshape(-1),
        ]
    )
    lines = -(-packed.size // (16 * width)) * 16
    packed = jnp.pad(packed, (0, lines * width - packed.size)).reshape(lines, width)
    shipped = jnp.concatenate([query_matrix, key_matrix, value_matrix, output_matrix, packed])
    arrived_all = [
        lax.all_to_all(block_input[t, :, 0], "exp", split_axis=1, concat_axis=0, tiled=True).reshape(slots, width)
        for t in range(mb)
    ]
    ready, (dense_full, table) = gather_all(shipped, arrived_all[0], n_exp, n_f, ex, fi, share)
    table = table.reshape(owners, -1).astype(F32)
    cot = out_cotangent[:, :, 0].reshape(mb, le, rows, width)
    other = (1 - (fi // 2) % 2).astype(jnp.int32).reshape(1)
    cot_far = both_groups(after(cot, ready), n_f)
    w_near = lax.ppermute(after(jnp.concatenate([expert_in, expert_out]), ready), "fsdp", near)
    block_rows = block_input[:, :, 0].reshape(mb, le, rows, width)

    small = jnp.stack(
        [table[:, i * share : (i + 1) * share].reshape(-1) for i in range(7)] + [jnp.zeros((width,), F32)]
    )
    at = 7 * share
    table = table.reshape(n_exp, n_f, -1)
    mine = pick(table, ex, 0)
    bias_out = mine[:, at : at + expert_out_bias.size].reshape(n_f, le, -1).transpose(1, 0, 2).reshape(le, width)
    at += expert_out_bias.size
    bias_in = mine[:, at : at + le * hidden].reshape(n_f, le, hidden)
    bias_in = jnp.concatenate([pick(bias_in, fi, 0), pick(bias_in, fi ^ 1, 0)], axis=1)[:, None, :]
    at += le * hidden
    my_counts = table[:, :, at : at + counts.size].reshape(n_exp, n_f, mb, n_exp, le)
    my_counts = pick(my_counts, ex, 3)

    def fill(group):
        count = pick(my_counts, group, 1).transpose(1, 2, 0)[:, :, :, None]
        return (jnp.arange(cap, dtype=F32) < count).astype(F32).reshape(mb, le, rows, 1)

    fill_own, fill_far = fill(fi), fill(fi ^ 2)

    saved, back_rows, normed_two = [], [], []
    for t in range(mb):
        placed, kept = attention_forward(arrived_all[t], slot_ids[t], seq_lengths[t, 0], dense_full, small)
        saved.append(kept)
        back_rows.append(
            lax.all_to_all(
                placed.reshape(experts, cap, width), "exp", split_axis=0, concat_axis=1, tiled=True
            ).reshape(le, rows, width)
        )
        normed_two.append(mixed_norm(t, block_rows, back_rows[t], small[5:6], small[6:7]))
    normed_far = [lax.ppermute(normed_two[0], "fsdp", far)[None]]
    for t in range(1, mb):
        rows_sent, cot_far = lax.optimization_barrier((normed_two[t], cot_far))
        normed_far.append(lax.ppermute(rows_sent, "fsdp", far)[None])

    ffn, before = [], None
    for t in range(mb):
        ffn.append(
            expert_step(
                t, other, normed_two[t], normed_far[t], cot, cot_far, (fill_own[t], fill_far[t]),
                expert_in, expert_out, w_near, bias_in, before,
            )
        )
        before = ffn[t][4:]
    gx_far = [lax.ppermute(ffn[0][3], "fsdp", far)[None]]
    out_far = [both_groups(ffn[t][1], n_f) for t in range(mb - 1)]
    for t in range(1, mb):
        gx_far.append(both_groups(after(ffn[t][3], gx_far[t - 1]), n_f))
    dwi_own, dwo_own, dw_near, db, dbo = before
    dbo = dbo[:, 0]
    vectors = jnp.concatenate([db[:, 0, hidden:], dbo], axis=1)

    dw_got = lax.ppermute(dw_near, "fsdp", near)
    input_grads, terms, small_total = [], [], None
    for t in range(mb):
        got = gx_far[t]
        if t == mb - 1:
            got, outs, placed_back = lax.optimization_barrier((got, ffn[t][1], placed_back))
            out_far.append(both_groups(outs, n_f))
        grad_mixed, to_send, norm_sums = mixed_back(
            t, other, block_rows, back_rows[t], ffn[t][2], got, cot, fill_own[t], small[5:6]
        )
        grad_arrived = lax.all_to_all(
            to_send.reshape(le, sources, cap, width), "exp", split_axis=1, concat_axis=0, tiled=True
        ).reshape(slots, width)
        placed_back, keep, give, sums = attention_backward(
            grad_arrived, slot_ids[t], seq_lengths[t, 0], core, dense_full, small, saved[t], owners, n_f
        )
        returned = lax.all_to_all(
            placed_back.reshape(experts, cap, width), "exp", split_axis=0, concat_axis=1, tiled=True
        ).reshape(le, rows, width)
        input_grads.append(
            (grad_mixed + returned.astype(F32)).astype(BF).reshape(le, 1, sources, cap, width)
        )
        sums = jnp.concatenate([sums[:5], norm_sums[:2], norm_sums[7:]])
        terms += list(keep) + [lax.ppermute(part, "exp", crossed(n_exp, 1)) for part in give]
        small_total = sums if t == 0 else small_total + sums

    sums_got = lax.ppermute(small_total, "exp", crossed(n_exp, 1))
    blocks = add_dense(terms, small_total, sums_got, chip, n_f)
    got = [lax.ppermute(blocks[k], "exp", crossed(n_exp, 2 * k)) for k in range(1, n_exp // 2)]
    keep, give, sums = add_plane((fi // 2) % 2, blocks[0], got)
    far_got = lax.ppermute(give, "fsdp", far)
    outputs = []
    for t in range(mb):
        mixed = block_rows[t].astype(F32) + back_rows[t].astype(F32)
        ffn_out = ffn[t][0].astype(F32) + pick(out_far[t], other[0], 0).astype(F32) + bias_out[:, None, :]
        outputs.append(
            ((mixed + ffn_out) * fill_own[t]).astype(BF).reshape(le, 1, sources, cap, width)
        )
    outputs = jnp.stack(outputs)
    half = keep.shape[0]
    keep = keep + far_got[:half].astype(F32)
    sums = sums + far_got[half:].astype(F32)
    pairs = keep.reshape(2, 4 * share, width)
    ride = jnp.pad(vectors, ((0, 0), (0, -vectors.shape[1] % width))).reshape(-1, width)
    give = jnp.concatenate([pick(pairs, 1 - fi % 2, 0), sums, ride]).astype(BF)
    give, outputs = lax.optimization_barrier((give, outputs))
    near_got = lax.ppermute(give, "fsdp", near).astype(F32)
    total = pick(pairs, fi % 2, 0) + near_got[: 4 * share]
    sums = sums + near_got[4 * share : 4 * share + 16]
    vectors_got = near_got[4 * share + 16 :].reshape(le, -1)[:, : vectors.shape[1]]
    grad_in, grad_out = add_near(dwi_own, dwo_own, dw_got)
    dense = total.reshape(4, share, width)
    smalls = lax.dynamic_slice_in_dim(sums, (ex * n_f + fi) * share, share, 1)

    grad_in_bias = db[:, 0, :hidden] + vectors_got[:, :hidden]
    grad_out_bias = lax.dynamic_slice_in_dim(
        dbo + vectors_got[:, hidden:], fi * (width // n_f), width // n_f, 1
    )
    return (
        outputs,
        jnp.stack(input_grads),
        smalls[0],
        smalls[1],
        dense[0],
        smalls[2],
        dense[1],
        dense[2],
        smalls[3],
        dense[3],
        smalls[4],
        smalls[5],
        smalls[6],
        grad_in,
        grad_in_bias,
        grad_out,
        grad_out_bias,
    )


def solution(mesh):
    rows, dense, vec = (
        P(None, "exp", "fsdp", None, None, None),
        P(("exp", "fsdp"), None),
        P(("exp", "fsdp")),
    )
    experts = (P("exp", None, "fsdp"), P("exp", "fsdp"), P("exp", "fsdp", None), P("exp", "fsdp"))
    return jax.shard_map(
        body,
        mesh=mesh,
        in_specs=(
            rows,
            P(None, ("exp", "fsdp"), None, None),
            P(None, ("exp", "fsdp")),
            vec,
            vec,
            dense,
            vec,
            dense,
            dense,
            vec,
            dense,
            vec,
            vec,
            vec,
        )
        + experts
        + (rows,),
        out_specs=(rows, rows, vec, vec, dense, vec, dense, dense, vec, dense, vec, vec, vec) + experts,
        check_vma=False,
    )
```
